32 devices in a mesh: group: 2 (over y), dp: 4 (over z), adapter: 4 (over x, core).
Axes of the slice: x: 2, y: 2, z: 4, core: 2. Of those that a mesh axis runs over, the one named last changes fastest.
Arguments:
- layer_activation_matrix: bfloat16 [8192, 5120], P(('group', 'dp', 'adapter')), parts along dimension 0, may hold values from -6 to 6
- loss_sensitivity: bfloat16 [8192, 1024], P(('group', 'dp', 'adapter')), parts along dimension 0, may hold values from -6 to 6
- fixed_projection_matrix: bfloat16 [5120, 1024], P('dp'), may hold values from -0.078125 to 0.078125
- plugin_factor_matrices: bfloat16 [512, 16, 6144], P('adapter', None, 'dp')
- element_slot_position: int32 [8192], P(('group', 'dp', 'adapter')), parts along dimension 0, may hold values from 0 to 511, as said below
- segment_plugin_choice: int32 [128], P(('group', 'dp', 'adapter')), parts along dimension 0, may hold values from 0 to 511, as said below
Outputs:
- input_token_gradient: bfloat16 [8192, 5120], P(('group', 'dp', 'adapter')), parts along dimension 0
- adapter_grad: float32 [1024, 16, 6144], P(('group', 'adapter'), None, 'dp'), parts along dimension 0
The draws below stay inside these ranges and needn't reach their ends.
There are 2 independent parts, one for each index of `group`. The reference program is written for one: setup_inputs(seed, part) draws one part's arguments, and reference() takes and returns one part's arrays. A program takes and returns all parts, laid end to end along the dimension named above; an argument that names none is the same for every part. Nothing has to cross between parts.
Inputs may be any that keep to these rules, and one draw needn't show every extreme that they name: `element_slot_position`: each device's tokens take distinct rows of its 4 blocks of 128 rows; every block holds 1 to 128 tokens, placed in its last rows, and every device has one full block. `segment_plugin_choice`: blocks of one device may name the same adapter.
All inputs are finite; a program needn't handle non-finite values.
Results may differ from the reference program's by a relative error of at most 0.005.
Values may be sent and summed in bfloat16 or wider, within the bound.
A program may use at most 128 MiB of HBM per device.

```python
import jax
import jax.numpy as jnp
from jax import lax

D = 5120
KV = 1024
R = 16
ADAPTERS = 512
BLK = 128
TOK_DEV = 256
NBLK = 4
TOKENS = 4096
BLOCKS = 64


def draw_plugin_factor_matrices(key, part):
    key = jax.random.fold_in(key, 3)
    values = jax.random.normal(key, (ADAPTERS, R, D + KV), jnp.float32)
    column = jnp.arange(D + KV)
    factor = jnp.where(column < D, D ** (-0.5), KV ** (-0.5))
    return (values * factor[None, None, :]).astype(jnp.bfloat16)


def draw_element_slot_position(key, part):
    key = jax.random.fold_in(key, 1)
    key_counts, key_order, key_tokens = jax.random.split(key, 3)
    devices_part = TOKENS // TOK_DEV
    remainder = TOK_DEV - BLK
    floor_count = max(1, (remainder - BLK + NBLK - 3) // (NBLK - 2))
    spare_count = remainder - (NBLK - 1) * floor_count
    selected_adapter = jax.random.randint(key_counts, (devices_part, spare_count), 0, NBLK - 1)
    extra_rows = jnp.sum((selected_adapter[:, :, None] == jnp.arange(NBLK - 1)[None, None, :]).astype(jnp.int32), axis=1)
    counts = jnp.concatenate([jnp.full((devices_part, 1), BLK, jnp.int32), floor_count + extra_rows], axis=1)
    counts = jax.vmap(jax.random.permutation)(jax.random.split(key_order, devices_part), counts)
    position = jnp.arange(NBLK * BLK)
    filled = (position % BLK)[None, :] >= BLK - counts[:, position // BLK]
    ranking = jnp.argsort(1 - filled.astype(jnp.int32), axis=1, stable=True)[:, :TOK_DEV]
    shuffled = jax.vmap(jax.random.permutation)(jax.random.split(key_tokens, devices_part), ranking)
    return shuffled.reshape(TOKENS).astype(jnp.int32)


def draw_segment_plugin_choice(key, part):
    key = jax.random.fold_in(key, 2)
    key_skew, key_label, key_first, key_second = jax.random.split(key, 4)
    draws_three = jax.random.randint(key_skew, (3, BLOCKS), 0, ADAPTERS)
    skewed = jnp.min(draws_three, axis=0)
    labels = jax.random.permutation(key_label, ADAPTERS)
    adapter_ids = labels[skewed]
    first_spot = jax.random.randint(key_first, (), 0, BLOCKS)
    second_spot = (first_spot + jax.random.randint(key_second, (), 1, BLOCKS)) % BLOCKS
    adapter_ids = adapter_ids.at[first_spot].set(ADAPTERS - 1).at[second_spot].set(0)
    return adapter_ids.astype(jnp.int32)


def steps_of(key, shape, cuts, smallest, high):
    gain = 1.0
    for dim, blocks in cuts:
        heights = jax.random.uniform(jax.random.fold_in(jax.random.fold_in(key, 6), dim), (blocks,), jnp.float32, smallest / len(cuts), high / len(cuts))
        gain = gain * jnp.repeat(jnp.exp(heights), shape[dim] // blocks).reshape((-1,) + (1,) * (len(shape) - 1 - dim))
    return gain


def noise(key, extent, scale, bound, shards=(), held_as=jnp.bfloat16):
    factor_of = steps_of(key, extent, shards, -0.22, 0.18) if shards else 1.0
    drawn = jax.random.normal(key, extent, jnp.float32) * scale * factor_of
    return jnp.minimum(jnp.maximum(drawn, -bound), bound).astype(held_as)


def setup_inputs(seed: int = 0, part: int = 0) -> dict:
    keys = jax.random.split(jax.random.key(seed), 7)
    part_keys = jax.random.split(jax.random.fold_in(keys[6], part), 7)
    layer_activation_matrix = noise(part_keys[0], (TOKENS, D), 1.0, 6.0, ((0, 16),))
    loss_sensitivity = noise(part_keys[1], (TOKENS, KV), 1.0, 6.0, ((0, 16),))
    fixed_projection_matrix = noise(keys[2], (D, KV), D ** -0.5, 0.078125, ((0, 4),))
    plugin_factor_matrices = draw_plugin_factor_matrices(jax.random.fold_in(keys[6], 71), part)
    element_slot_position = draw_element_slot_position(jax.random.fold_in(jax.random.fold_in(keys[6], part), 71), part)
    segment_plugin_choice = draw_segment_plugin_choice(jax.random.fold_in(jax.random.fold_in(keys[6], part), 71), part)
    return {"layer_activation_matrix": layer_activation_matrix, "loss_sensitivity": loss_sensitivity, "fixed_projection_matrix": fixed_projection_matrix, "plugin_factor_matrices": plugin_factor_matrices, "element_slot_position": element_slot_position, "segment_plugin_choice": segment_plugin_choice}


adapter_scale = 2.0


def reference(layer_activation_matrix, loss_sensitivity, fixed_projection_matrix, plugin_factor_matrices, element_slot_position, segment_plugin_choice):
    device_of = jnp.arange(TOKENS, dtype=jnp.int32) // TOK_DEV
    adapter_of = segment_plugin_choice[(device_of * NBLK + element_slot_position // BLK).astype(jnp.int32)]
    frozen_weight = jnp.dot(loss_sensitivity, fixed_projection_matrix.T, preferred_element_type=jnp.float32)
    frozen_weight = lax.optimization_barrier(frozen_weight.astype(jnp.bfloat16)).astype(jnp.float32)
    parameter_sequence = plugin_factor_matrices.astype(jnp.float32)

    def visit(loop_carry, inputs):
        rows_x, rows_g, selected_adapter = inputs
        x_float = rows_x.astype(jnp.float32)
        g_float = rows_g.astype(jnp.float32)
        picked = parameter_sequence[selected_adapter]
        down_weight_rows = picked[:, :, :D]
        up_rows = picked[:, :, D:]
        low_in = jnp.einsum("td,trd->tr", x_float, down_weight_rows)
        low_in = lax.optimization_barrier(low_in.astype(jnp.bfloat16)).astype(jnp.float32)
        low_rank_output = jnp.einsum("tk,trk->tr", g_float, up_rows)
        low_rank_output = lax.optimization_barrier(low_rank_output.astype(jnp.bfloat16)).astype(jnp.float32)
        additional_input_gradient = adapter_scale * jnp.einsum("yh,yhl->yl", low_rank_output, down_weight_rows)
        gradient_list = jnp.concatenate([low_rank_output[:, :, None] * x_float[:, None, :], low_in[:, :, None] * g_float[:, None, :]], axis=2)
        loop_carry = loop_carry.at[selected_adapter].add(adapter_scale * gradient_list)
        return loop_carry, additional_input_gradient

    zero_grad = jnp.zeros((ADAPTERS, R, D + KV), jnp.float32)
    adapter_grad, extra = lax.scan(visit, zero_grad, (layer_activation_matrix.reshape(-1, TOK_DEV, D), loss_sensitivity.reshape(-1, TOK_DEV, KV), adapter_of.reshape(-1, TOK_DEV)))
    input_token_gradient = (frozen_weight + extra.reshape(TOKENS, D)).astype(jnp.bfloat16)
    return input_token_gradient, adapter_grad
```

```python
import functools

import jax
import jax.numpy as jnp
from jax import lax
from jax.experimental import pallas as pl
from jax.experimental.pallas import tpu as pltpu
from jax.sharding import PartitionSpec as P

BLK = 128

adapter_scale = 2.0
MESH = pl.DeviceIdType.MESH
VMEM_LIMIT = 48 * 1024 * 1024


def remote(src, dst, send, recv, **where):
    return pltpu.make_async_remote_copy(
        src_ref=src, dst_ref=dst, send_sem=send, recv_sem=recv, device_id=where, device_id_type=MESH
    )


def greet(peers):
    barrier = pltpu.get_barrier_semaphore()
    nd = lax.axis_size("dp")
    me = lax.axis_index("dp")

    @pl.loop(1, nd)
    def _(o):
        pl.semaphore_signal(barrier, inc=1, device_id={"dp": lax.rem(me + o, nd)}, device_id_type=MESH)

    for peer in peers:
        pl.semaphore_signal(barrier, inc=1, device_id=peer, device_id_type=MESH)
    pl.semaphore_wait(barrier, nd - 1 + len(peers))


def fetch_kernel(
    nb, ids, cat, weight, fetched, gathered, pieces, from_core, from_x,
    s1, r1, s2, r2, s3, r3, sz, rz, sx, rx, sy, ry, sc, rc, local_sem,
):
    nd = lax.axis_size("dp")
    me = lax.axis_index("dp")
    g = lax.axis_index("group")
    a = lax.axis_index("adapter")
    x, c = a // 2, a % 2
    core = x * 2 + (1 - c)
    other = (1 - x) * 2 + c
    held, rank, _ = cat.shape
    greet([{"adapter": core}, {"adapter": other}, {"group": 1 - g}])

    def w_z(o):
        return remote(weight.at[c, g, x], gathered.at[me, c, g, x], sz.at[o], rz.at[o], dp=lax.rem(me + o, nd))

    def w_x(o):
        s = lax.rem(me + nd - o, nd)
        return remote(gathered.at[s, c, g, x], gathered.at[s, c, g, x], sx.at[o], rx.at[o], adapter=other)

    def w_y(o):
        s = lax.rem(me + nd - o, nd)
        return remote(gathered.at[s, c, g], gathered.at[s, c, g], sy.at[o], ry.at[o], group=1 - g)

    def w_c(o):
        s = lax.rem(me + nd - o, nd)
        return remote(gathered.at[s, c], gathered.at[s, c], sc.at[o], rc.at[o], adapter=core)

    def f_core(o):
        d = lax.rem(me + o, nd)
        return remote(pieces.at[d, 1 - c], from_core.at[d], s1.at[o], r1.at[o], adapter=core)

    def f_x(o):
        d = lax.rem(me + o, nd)
        return remote(pieces.at[d, c, 1 - x], from_x.at[d], s2.at[o], r2.at[o], adapter=other)

    def f_z(o):
        d = lax.rem(me + o, nd)
        return remote(pieces.at[d, c, x], fetched.at[me], s3.at[o], r3.at[o], dp=d)

    @pl.loop(1, nd)
    def _(o):
        w_z(o).start()

    own = pltpu.make_async_copy(weight, gathered.at[me], local_sem.at[0])
    own.start()

    @pl.loop(0, nd)
    def _(i):
        o = lax.rem(i + 1, nd)
        d = lax.rem(me + o, nd)

        @pl.loop(0, 4)
        def _(q):
            xx, cc = q // 2, q % 2
            for k in range(nb):
                local_id = ids[(d * 4 + q) * nb + k] - a * held
                valid = (local_id >= 0) & (local_id < held)
                row = cat[jnp.clip(local_id, 0, held - 1)]
                pieces[d, cc, xx, k * rank : (k + 1) * rank, :] = jnp.where(valid, row, jnp.zeros_like(row))

        f_core(o).start()

    @pl.loop(0, nd)
    def _(i):
        o = lax.rem(i + 1, nd)
        d = lax.rem(me + o, nd)
        f_core(o).wait_recv()
        pieces[d, c] += from_core[d]
        f_x(o).start()

    def x_done(o):
        d = lax.rem(me + o, nd)
        f_x(o).wait_recv()
        pieces[d, c, x] += from_x[d]

    @pl.loop(1, nd)
    def _(o):
        x_done(o)
        f_z(o).start()
        w_z(o).wait_recv()
        w_x(o).start()

    x_done(0)
    mine = pltpu.make_async_copy(pieces.at[me, c, x], fetched.at[me], local_sem.at[1])
    mine.start()

    @pl.loop(1, nd)
    def _(o):
        w_x(o).wait_recv()
        w_y(o).start()

    @pl.loop(1, nd)
    def _(o):
        w_y(o).wait_recv()
        w_c(o).start()

    @pl.loop(1, nd)
    def _(o):
        f_z(o).wait()
        w_z(o).wait_send()
        w_x(o).wait_send()
        w_y(o).wait_send()
        w_c(o).wait()

    @pl.loop(0, nd)
    def _(o):
        f_core(o).wait_send()
        f_x(o).wait_send()

    own.wait()
    mine.wait()


def fetch(ids, catalog, weight, nd, nb):
    held, rank, width = catalog.shape
    rows, kv = weight.shape
    weight = weight.reshape(2, 2, 2, rows // 8, kv)
    dma = pltpu.SemaphoreType.DMA((nd,))
    return pl.pallas_call(
        functools.partial(fetch_kernel, nb),
        out_shape=(
            jax.ShapeDtypeStruct((nd, nb * rank, width), jnp.bfloat16),
            jax.ShapeDtypeStruct((nd, 2, 2, 2, rows // 8, kv), jnp.bfloat16),
        ),
        in_specs=[
            pl.BlockSpec(memory_space=pltpu.SMEM),
            pl.BlockSpec(memory_space=pltpu.VMEM),
            pl.BlockSpec(memory_space=pl.ANY),
        ],
        out_specs=(pl.BlockSpec(memory_space=pl.ANY), pl.BlockSpec(memory_space=pl.ANY)),
        scratch_shapes=[
            pltpu.VMEM((nd, 2, 2, nb * rank, width), jnp.bfloat16),
            pltpu.VMEM((nd, 2, nb * rank, width), jnp.bfloat16),
            pltpu.VMEM((nd, nb * rank, width), jnp.bfloat16),
        ]
        + [dma] * 14
        + [pltpu.SemaphoreType.DMA((2,))],
        compiler_params=pltpu.CompilerParams(
            collective_id=0, has_side_effects=True, vmem_limit_bytes=VMEM_LIMIT
        ),
    )(ids, catalog, weight)


def exchange_kernel(grads, out, sz, rz, sx, rx, sc, rc, local_sem):
    nd = lax.axis_size("dp")
    me = lax.axis_index("dp")
    a = lax.axis_index("adapter")
    x, c = a // 2, a % 2
    core = x * 2 + (1 - c)
    other = (1 - x) * 2 + c
    greet([{"adapter": core}, {"adapter": other}])

    def g_z(o):
        d = lax.rem(me + o, nd)
        return remote(grads.at[d], out.at[me, x, c], sz.at[o], rz.at[o], dp=d)

    def g_x(o):
        s = lax.rem(me + nd - o, nd)
        return remote(out.at[s, x, c], out.at[s, x, c], sx.at[o], rx.at[o], adapter=other)

    def g_c(o):
        s = lax.rem(me + nd - o, nd)
        return remote(out.at[s, :, c], out.at[s, :, c], sc.at[o], rc.at[o], adapter=core)

    @pl.loop(1, nd)
    def _(o):
        g_z(o).start()

    own = pltpu.make_async_copy(grads.at[me], out.at[me, x, c], local_sem)
    own.start()
    own.wait()
    g_x(0).start()

    @pl.loop(1, nd)
    def _(o):
        g_z(o).wait_recv()
        g_x(o).start()

    @pl.loop(0, nd)
    def _(o):
        g_x(o).wait_recv()
        g_c(o).start()

    @pl.loop(1, nd)
    def _(o):
        g_z(o).wait_send()

    @pl.loop(0, nd)
    def _(o):
        g_x(o).wait_send()
        g_c(o).wait()


def exchange(grads):
    nd, rows, width = grads.shape
    dma = pltpu.SemaphoreType.DMA((nd,))
    return pl.pallas_call(
        exchange_kernel,
        out_shape=jax.ShapeDtypeStruct((nd, 2, 2, rows, width), jnp.bfloat16),
        in_specs=[pl.BlockSpec(memory_space=pl.ANY)],
        out_specs=pl.BlockSpec(memory_space=pl.ANY),
        scratch_shapes=[dma] * 6 + [pltpu.SemaphoreType.DMA],
        compiler_params=pltpu.CompilerParams(
            collective_id=1, has_side_effects=True, vmem_limit_bytes=VMEM_LIMIT
        ),
    )(grads)


def place_kernel(ids, rows, out):
    count = out.shape[0]
    base = pl.program_id(0) * count
    out[...] = jnp.zeros_like(out)

    @pl.loop(0, rows.shape[0])
    def _(s):
        target = ids[s] - base

        @pl.when((target >= 0) & (target < count))
        def _():
            out[target] += rows[s].astype(jnp.float32)


def place(ids, rows, held):
    total, rank, width = rows.shape
    step = 16
    return pl.pallas_call(
        place_kernel,
        out_shape=jax.ShapeDtypeStruct((held, rank, width), jnp.float32),
        grid_spec=pltpu.PrefetchScalarGridSpec(
            num_scalar_prefetch=1,
            grid=(held // step,),
            in_specs=[pl.BlockSpec((total, rank, width), lambda i, ids: (0, 0, 0))],
            out_specs=pl.BlockSpec((step, rank, width), lambda i, ids: (i, 0, 0)),
        ),
        compiler_params=pltpu.CompilerParams(vmem_limit_bytes=VMEM_LIMIT),
    )(ids, rows)


def local(
    layer_activation_matrix,
    loss_sensitivity,
    fixed_projection_matrix,
    plugin_factor_matrices,
    element_slot_position,
    segment_plugin_choice,
):
    token_count, model_width = layer_activation_matrix.shape
    block_count = segment_plugin_choice.shape[0]
    held, rank, width = plugin_factor_matrices.shape
    nd = lax.axis_size("dp")
    owner_index = lax.axis_index("adapter")
    ids = lax.all_gather(segment_plugin_choice, ("dp", "adapter"), axis=0, tiled=True)
    fetched, weight = fetch(ids, plugin_factor_matrices, fixed_projection_matrix, nd, block_count)
    weight = weight.reshape(model_width, loss_sensitivity.shape[1])
    columns = block_count * rank
    factors = jnp.transpose(fetched, (1, 0, 2)).reshape(columns, nd * width)
    down, up = factors[:, :model_width], factors[:, model_width:]
    owned = (element_slot_position // BLK)[:, None] == (jnp.arange(columns) // rank)[None, :]

    def dot(lhs, rhs, left, right):
        return lax.dot_general(
            lhs, rhs, (((left,), (right,)), ((), ())), preferred_element_type=jnp.float32
        )

    low_in = jnp.where(owned, dot(layer_activation_matrix, down, 1, 1).astype(jnp.bfloat16), 0)
    low_out = jnp.where(owned, dot(loss_sensitivity, up, 1, 1).astype(jnp.bfloat16), 0)
    down_grad = (adapter_scale * dot(low_out, layer_activation_matrix, 0, 0)).astype(jnp.bfloat16)
    up_grad = (adapter_scale * dot(low_in, loss_sensitivity, 0, 0)).astype(jnp.bfloat16)
    grads = jnp.concatenate([down_grad, up_grad], axis=1).reshape(columns, nd, width)
    everyone = exchange(jnp.transpose(grads, (1, 0, 2)))
    adapter_grad = place(
        ids - owner_index * held, everyone.reshape(ids.shape[0], rank, width), held
    )
    frozen = dot(loss_sensitivity, weight, 1, 1).astype(jnp.bfloat16)
    frozen = lax.optimization_barrier(frozen).astype(jnp.float32)
    input_token_gradient = (frozen + adapter_scale * dot(low_out, down, 1, 0)).astype(jnp.bfloat16)
    return (input_token_gradient, adapter_grad)


def solution(mesh):
    return jax.shard_map(
        local,
        mesh=mesh,
        in_specs=(
            P(("group", "dp", "adapter"), None),
            P(("group", "dp", "adapter"), None),
            P("dp", None),
            P("adapter", None, "dp"),
            P(("group", "dp", "adapter")),
            P(("group", "dp", "adapter")),
        ),
        out_specs=(P(("group", "dp", "adapter"), None), P(("group", "adapter"), None, "dp")),
        check_vma=False,
    )
```

```python
import functools

import jax
import jax.numpy as jnp
from jax import lax
from jax.experimental import pallas as pl
from jax.experimental.pallas import tpu as pltpu
from jax.sharding import PartitionSpec as P

BLK = 128

adapter_scale = 2.0
MESH = pl.DeviceIdType.MESH
VMEM_LIMIT = 48 * 1024 * 1024


def remote(src, dst, send, recv, **where):
    return pltpu.make_async_remote_copy(
        src_ref=src, dst_ref=dst, send_sem=send, recv_sem=recv, device_id=where, device_id_type=MESH
    )


def greet(peers):
    barrier = pltpu.get_barrier_semaphore()
    nd = lax.axis_size("dp")
    me = lax.axis_index("dp")

    @pl.loop(1, nd)
    def _(o):
        pl.semaphore_signal(barrier, inc=1, device_id={"dp": lax.rem(me + o, nd)}, device_id_type=MESH)

    for peer in peers:
        pl.semaphore_signal(barrier, inc=1, device_id=peer, device_id_type=MESH)
    pl.semaphore_wait(barrier, nd - 1 + len(peers))


def fetch_kernel(
    nb, ids, cat, weight, fetched, gathered, pieces, from_core, from_x,
    s1, r1, s2, r2, s3, r3, sz, rz, sx, rx, sy, ry, sc, rc, local_sem,
):
    nd = lax.axis_size("dp")
    me = lax.axis_index("dp")
    g = lax.axis_index("group")
    a = lax.axis_index("adapter")
    x, c = a // 2, a % 2
    core = x * 2 + (1 - c)
    other = (1 - x) * 2 + c
    held, rank, _ = cat.shape
    greet([{"adapter": core}, {"adapter": other}, {"group": 1 - g}])

    def w_z(o):
        return remote(weight.at[c, g, x], gathered.at[me, c, g, x], sz.at[o], rz.at[o], dp=lax.rem(me + o, nd))

    def w_x(o):
        s = lax.rem(me + nd - o, nd)
        return remote(gathered.at[s, c, g, x], gathered.at[s, c, g, x], sx.at[o], rx.at[o], adapter=other)

    def w_y(o):
        s = lax.rem(me + nd - o, nd)
        return remote(gathered.at[s, c, g], gathered.at[s, c, g], sy.at[o], ry.at[o], group=1 - g)

    def w_c(o):
        s = lax.rem(me + nd - o, nd)
        return remote(gathered.at[s, c], gathered.at[s, c], sc.at[o], rc.at[o], adapter=core)

    def f_core(o):
        d = lax.rem(me + o, nd)
        return remote(pieces.at[d, 1 - c], from_core.at[d], s1.at[o], r1.at[o], adapter=core)

    def f_x(o):
        d = lax.rem(me + o, nd)
        return remote(pieces.at[d, c, 1 - x], from_x.at[d], s2.at[o], r2.at[o], adapter=other)

    def f_z(o):
        d = lax.rem(me + o, nd)
        return remote(pieces.at[d, c, x], fetched.at[me], s3.at[o], r3.at[o], dp=d)

    @pl.loop(1, nd)
    def _(o):
        w_z(o).start()

    own = pltpu.make_async_copy(weight, gathered.at[me], local_sem.at[0])
    own.start()

    @pl.loop(0, nd)
    def _(i):
        o = lax.rem(i + 1, nd)
        d = lax.rem(me + o, nd)

        @pl.loop(0, 4)
        def _(q):
            xx, cc = q // 2, q % 2
            for k in range(nb):
                local_id = ids[(d * 4 + q) * nb + k] - a * held
                valid = (local_id >= 0) & (local_id < held)
                row = cat[jnp.clip(local_id, 0, held - 1)]
                pieces[d, cc, xx, k * rank : (k + 1) * rank, :] = jnp.where(valid, row, jnp.zeros_like(row))

        f_core(o).start()

    @pl.loop(0, nd)
    def _(i):
        o = lax.rem(i + 1, nd)
        d = lax.rem(me + o, nd)
        f_core(o).wait_recv()
        pieces[d, c] += from_core[d]
        f_x(o).start()

    def x_done(o):
        d = lax.rem(me + o, nd)
        f_x(o).wait_recv()
        pieces[d, c, x] += from_x[d]

    @pl.loop(1, nd)
    def _(o):
        x_done(o)
        f_z(o).start()
        w_z(o).wait_recv()
        w_x(o).start()

    x_done(0)
    mine = pltpu.make_async_copy(pieces.at[me, c, x], fetched.at[me], local_sem.at[1])
    mine.start()

    @pl.loop(1, nd)
    def _(o):
        w_x(o).wait_recv()
        w_y(o).start()

    @pl.loop(1, nd)
    def _(o):
        w_y(o).wait_recv()
        w_c(o).start()

    @pl.loop(1, nd)
    def _(o):
        f_z(o).wait()
        w_z(o).wait_send()
        w_x(o).wait_send()
        w_y(o).wait_send()
        w_c(o).wait()

    @pl.loop(0, nd)
    def _(o):
        f_core(o).wait_send()
        f_x(o).wait_send()

    own.wait()
    mine.wait()


def fetch(ids, catalog, weight, nd, nb):
    held, rank, width = catalog.shape
    rows, kv = weight.shape
    weight = weight.reshape(2, 2, 2, rows // 8, kv)
    dma = pltpu.SemaphoreType.DMA((nd,))
    return pl.pallas_call(
        functools.partial(fetch_kernel, nb),
        out_shape=(
            jax.ShapeDtypeStruct((nd, nb * rank, width), jnp.bfloat16),
            jax.ShapeDtypeStruct((nd, 2, 2, 2, rows // 8, kv), jnp.bfloat16),
        ),
        in_specs=[
            pl.BlockSpec(memory_space=pltpu.SMEM),
            pl.BlockSpec(memory_space=pltpu.VMEM),
            pl.BlockSpec(memory_space=pl.ANY),
        ],
        out_specs=(pl.BlockSpec(memory_space=pl.ANY), pl.BlockSpec(memory_space=pl.ANY)),
        scratch_shapes=[
            pltpu.VMEM((nd, 2, 2, nb * rank, width), jnp.bfloat16),
            pltpu.VMEM((nd, 2, nb * rank, width), jnp.bfloat16),
            pltpu.VMEM((nd, nb * rank, width), jnp.bfloat16),
        ]
        + [dma] * 14
        + [pltpu.SemaphoreType.DMA((2,))],
        compiler_params=pltpu.CompilerParams(
            collective_id=0, has_side_effects=True, vmem_limit_bytes=VMEM_LIMIT
        ),
    )(ids, catalog, weight)


def exchange_kernel(grads, out, sz, rz, sx, rx, sc, rc, local_sem):
    nd = lax.axis_size("dp")
    me = lax.axis_index("dp")
    a = lax.axis_index("adapter")
    x, c = a // 2, a % 2
    core = x * 2 + (1 - c)
    other = (1 - x) * 2 + c
    greet([{"adapter": core}, {"adapter": other}])

    def g_z(o):
        d = lax.rem(me + o, nd)
        return remote(grads.at[d], out.at[me, x, c], sz.at[o], rz.at[o], dp=d)

    def g_x(o):
        s = lax.rem(me + nd - o, nd)
        return remote(out.at[s, x, c], out.at[s, x, c], sx.at[o], rx.at[o], adapter=other)

    def g_c(o):
        s = lax.rem(me + nd - o, nd)
        return remote(out.at[s, :, c], out.at[s, :, c], sc.at[o], rc.at[o], adapter=core)

    @pl.loop(1, nd)
    def _(o):
        g_z(o).start()

    own = pltpu.make_async_copy(grads.at[me], out.at[me, x, c], local_sem)
    own.start()
    own.wait()
    g_x(0).start()

    @pl.loop(1, nd)
    def _(o):
        g_z(o).wait_recv()
        g_x(o).start()

    @pl.loop(0, nd)
    def _(o):
        g_x(o).wait_recv()
        g_c(o).start()

    @pl.loop(1, nd)
    def _(o):
        g_z(o).wait_send()

    @pl.loop(0, nd)
    def _(o):
        g_x(o).wait_send()
        g_c(o).wait()


def exchange(grads):
    nd, rows, width = grads.shape
    dma = pltpu.SemaphoreType.DMA((nd,))
    return pl.pallas_call(
        exchange_kernel,
        out_shape=jax.ShapeDtypeStruct((nd, 2, 2, rows, width), jnp.bfloat16),
        in_specs=[pl.BlockSpec(memory_space=pl.ANY)],
        out_specs=pl.BlockSpec(memory_space=pl.ANY),
        scratch_shapes=[dma] * 6 + [pltpu.SemaphoreType.DMA],
        compiler_params=pltpu.CompilerParams(
            collective_id=1, has_side_effects=True, vmem_limit_bytes=VMEM_LIMIT
        ),
    )(grads)


def whole_kernel(
    nb, ids, cat, weight, tokens, cotangent, owned, gradient, out,
    pieces, from_core, from_x, fetched, gathered, frozen, factors, grads,
    s1, r1, s2, r2, s3, r3, sz, rz, sx, rx, sy, ry, sc, rc, gsz, grz, gsx, grx, gsc, grc, local_sem,
):
    nd = lax.axis_size("dp")
    me = lax.axis_index("dp")
    g = lax.axis_index("group")
    a = lax.axis_index("adapter")
    x, c = a // 2, a % 2
    core = x * 2 + (1 - c)
    other = (1 - x) * 2 + c
    held, rank, width = cat.shape
    model_width = tokens.shape[1]
    shard = model_width // nd
    greet([{"adapter": core}, {"adapter": other}, {"group": 1 - g}])

    def after(o):
        return lax.rem(me + o, nd)

    def before(o):
        return lax.rem(me + nd - o, nd)

    def w_z(o):
        return remote(weight.at[c, g, x], gathered.at[me, c, g, x], sz.at[o], rz.at[o], dp=after(o))

    def w_x(o):
        block = gathered.at[before(o), c, g, x]
        return remote(block, block, sx.at[o], rx.at[o], adapter=other)

    def w_y(o):
        block = gathered.at[before(o), c, g]
        return remote(block, block, sy.at[o], ry.at[o], group=1 - g)

    def w_c(o):
        block = gathered.at[before(o), c]
        return remote(block, block, sc.at[o], rc.at[o], adapter=core)

    def f_core(o):
        d = after(o)
        return remote(pieces.at[d, 1 - c], from_core.at[d], s1.at[o], r1.at[o], adapter=core)

    def f_x(o):
        d = after(o)
        return remote(pieces.at[d, c, 1 - x], from_x.at[d], s2.at[o], r2.at[o], adapter=other)

    def f_z(o):
        d = after(o)
        return remote(pieces.at[d, c, x], fetched.at[me], s3.at[o], r3.at[o], dp=d)

    def g_z(o):
        d = after(o)
        return remote(grads.at[d], out.at[me, x, c], gsz.at[o], grz.at[o], dp=d)

    def g_x(o):
        block = out.at[before(o), x, c]
        return remote(block, block, gsx.at[o], grx.at[o], adapter=other)

    def g_c(o):
        block = out.at[before(o), :, c]
        return remote(block, block, gsc.at[o], grc.at[o], adapter=core)

    def dot(lhs, rhs, left, right):
        return lax.dot_general(
            lhs, rhs, (((left,), (right,)), ((), ())), preferred_element_type=jnp.float32
        )

    def freeze(s):
        rows = gathered[s].reshape(shard, gathered.shape[-1])
        frozen[s] = dot(cotangent[...], rows, 1, 1).astype(jnp.bfloat16)

    @pl.loop(1, nd)
    def _(o):
        w_z(o).start()

    own = pltpu.make_async_copy(weight, gathered.at[me], local_sem.at[0])
    own.start()

    @pl.loop(0, nd)
    def _(i):
        o = lax.rem(i + 1, nd)
        d = after(o)

        @pl.loop(0, 4)
        def _(q):
            xx, cc = q // 2, q % 2
            for k in range(nb):
                local_id = ids[(d * 4 + q) * nb + k] - a * held
                valid = (local_id >= 0) & (local_id < held)
                row = cat[jnp.clip(local_id, 0, held - 1)]
                pieces[d, cc, xx, k * rank : (k + 1) * rank, :] = jnp.where(valid, row, jnp.zeros_like(row))

        f_core(o).start()

    @pl.loop(0, nd)
    def _(i):
        o = lax.rem(i + 1, nd)
        d = after(o)
        f_core(o).wait_recv()
        pieces[d, c] += from_core[d]
        f_x(o).start()

    def x_done(o):
        d = after(o)
        f_x(o).wait_recv()
        pieces[d, c, x] += from_x[d]

    @pl.loop(1, nd)
    def _(o):
        x_done(o)
        f_z(o).start()
        w_z(o).wait_recv()
        w_x(o).start()

    x_done(0)
    fetched[me] = pieces[me, c, x]
    own.wait()
    freeze(me)
    w_x(1).wait_recv()
    w_y(1).start()

    @pl.loop(1, nd)
    def _(o):
        f_z(o).wait_recv()

    for j in range(nd):
        factors[:, j * width : (j + 1) * width] = fetched[j]
    mask = owned[...] > 0
    low_out = dot(cotangent[...], factors[:, model_width:], 1, 1)
    low_out = jnp.where(mask, low_out, 0.0).astype(jnp.bfloat16)
    low_in = dot(tokens[...], factors[:, :model_width], 1, 1)
    low_in = jnp.where(mask, low_in, 0.0).astype(jnp.bfloat16)
    for j in range(nd):
        inner = min(max(model_width - j * width, 0), width)
        if inner:
            part = dot(low_out, tokens[:, j * width : j * width + inner], 0, 0)
            grads[j, :, :inner] = (adapter_scale * part).astype(jnp.bfloat16)
        if inner < width:
            start = j * width + inner - model_width
            part = dot(low_in, cotangent[:, start : start + width - inner], 0, 0)
            grads[j, :, inner:] = (adapter_scale * part).astype(jnp.bfloat16)

    @pl.loop(1, nd)
    def _(o):
        g_z(o).start()

    mine = pltpu.make_async_copy(grads.at[me], out.at[me, x, c], local_sem.at[1])
    mine.start()
    mine.wait()
    g_x(0).start()

    @pl.loop(2, nd)
    def _(o):
        w_x(o).wait_recv()
        w_y(o).start()

    @pl.loop(1, nd)
    def _(o):
        g_z(o).wait_recv()
        g_x(o).start()

    w_y(1).wait_recv()
    w_c(1).start()

    @pl.loop(0, nd)
    def _(o):
        g_x(o).wait_recv()
        g_c(o).start()

    @pl.loop(2, nd)
    def _(o):
        w_y(o).wait_recv()
        w_c(o).start()

    @pl.loop(1, nd)
    def _(o):
        w_c(o).wait_recv()
        freeze(before(o))

    for s in range(nd):
        columns = slice(s * shard, (s + 1) * shard)
        extra = dot(low_out, factors[:, columns], 1, 0)
        gradient[:, columns] = (frozen[s].astype(jnp.float32) + adapter_scale * extra).astype(jnp.bfloat16)

    @pl.loop(1, nd)
    def _(o):
        f_z(o).wait_send()
        w_z(o).wait_send()
        w_x(o).wait_send()
        w_y(o).wait_send()
        w_c(o).wait_send()
        g_z(o).wait_send()

    @pl.loop(0, nd)
    def _(o):
        f_core(o).wait_send()
        f_x(o).wait_send()
        g_x(o).wait_send()
        g_c(o).wait()


def whole(ids, catalog, weight, tokens, cotangent, owned, nd, nb):
    held, rank, width = catalog.shape
    rows, kv = weight.shape
    columns = nb * rank
    weight = weight.reshape(2, 2, 2, rows // 8, kv)
    dma = pltpu.SemaphoreType.DMA((nd,))
    vmem = pl.BlockSpec(memory_space=pltpu.VMEM)
    anywhere = pl.BlockSpec(memory_space=pl.ANY)
    return pl.pallas_call(
        functools.partial(whole_kernel, nb),
        out_shape=(
            jax.ShapeDtypeStruct(tokens.shape, jnp.bfloat16),
            jax.ShapeDtypeStruct((nd, 2, 2, columns, width), jnp.bfloat16),
        ),
        in_specs=[pl.BlockSpec(memory_space=pltpu.SMEM), vmem, anywhere, vmem, vmem, vmem],
        out_specs=(vmem, anywhere),
        scratch_shapes=[
            pltpu.VMEM((nd, 2, 2, columns, width), jnp.bfloat16),
            pltpu.VMEM((nd, 2, columns, width), jnp.bfloat16),
            pltpu.VMEM((nd, columns, width), jnp.bfloat16),
            pltpu.VMEM((nd, columns, width), jnp.bfloat16),
            pltpu.VMEM((nd, 2, 2, 2, rows // 8, kv), jnp.bfloat16),
            pltpu.VMEM((nd, tokens.shape[0], rows), jnp.bfloat16),
            pltpu.VMEM((columns, nd * width), jnp.bfloat16),
            pltpu.VMEM((nd, columns, width), jnp.bfloat16),
        ]
        + [dma] * 20
        + [pltpu.SemaphoreType.DMA((2,))],
        compiler_params=pltpu.CompilerParams(
            collective_id=2, has_side_effects=True, vmem_limit_bytes=VMEM_LIMIT
        ),
    )(ids, catalog, weight, tokens, cotangent, owned)


def place_kernel(ids, rows, out):
    count = out.shape[0]
    base = pl.program_id(0) * count
    out[...] = jnp.zeros_like(out)

    @pl.loop(0, rows.shape[0])
    def _(s):
        target = ids[s] - base

        @pl.when((target >= 0) & (target < count))
        def _():
            out[target] += rows[s].astype(jnp.float32)


def place(ids, rows, held):
    total, rank, width = rows.shape
    step = 16
    return pl.pallas_call(
        place_kernel,
        out_shape=jax.ShapeDtypeStruct((held, rank, width), jnp.float32),
        grid_spec=pltpu.PrefetchScalarGridSpec(
            num_scalar_prefetch=1,
            grid=(held // step,),
            in_specs=[pl.BlockSpec((total, rank, width), lambda i, ids: (0, 0, 0))],
            out_specs=pl.BlockSpec((step, rank, width), lambda i, ids: (i, 0, 0)),
        ),
        compiler_params=pltpu.CompilerParams(vmem_limit_bytes=VMEM_LIMIT),
    )(ids, rows)


def local(
    layer_activation_matrix,
    loss_sensitivity,
    fixed_projection_matrix,
    plugin_factor_matrices,
    element_slot_position,
    segment_plugin_choice,
):
    token_count, model_width = layer_activation_matrix.shape
    block_count = segment_plugin_choice.shape[0]
    held, rank, width = plugin_factor_matrices.shape
    nd = lax.axis_size("dp")
    owner_index = lax.axis_index("adapter")
    ids = lax.all_gather(segment_plugin_choice, ("dp", "adapter"), axis=0, tiled=True)
    columns = block_count * rank
    owned = (element_slot_position // BLK)[:, None] == (jnp.arange(columns) // rank)[None, :]
    if width % 128 == 0 and model_width // nd % 128 == 0:
        input_token_gradient, everyone = whole(
            ids,
            plugin_factor_matrices,
            fixed_projection_matrix,
            layer_activation_matrix,
            loss_sensitivity,
            owned.astype(jnp.float32),
            nd,
            block_count,
        )
        everyone = everyone.reshape(ids.shape[0], rank, width)
        return (input_token_gradient, place(ids - owner_index * held, everyone, held))
    fetched, weight = fetch(ids, plugin_factor_matrices, fixed_projection_matrix, nd, block_count)
    weight = weight.reshape(model_width, loss_sensitivity.shape[1])
    factors = jnp.transpose(fetched, (1, 0, 2)).reshape(columns, nd * width)
    down, up = factors[:, :model_width], factors[:, model_width:]

    def dot(lhs, rhs, left, right):
        return lax.dot_general(
            lhs, rhs, (((left,), (right,)), ((), ())), preferred_element_type=jnp.float32
        )

    low_in = jnp.where(owned, dot(layer_activation_matrix, down, 1, 1).astype(jnp.bfloat16), 0)
    low_out = jnp.where(owned, dot(loss_sensitivity, up, 1, 1).astype(jnp.bfloat16), 0)
    down_grad = (adapter_scale * dot(low_out, layer_activation_matrix, 0, 0)).astype(jnp.bfloat16)
    up_grad = (adapter_scale * dot(low_in, loss_sensitivity, 0, 0)).astype(jnp.bfloat16)
    grads = jnp.concatenate([down_grad, up_grad], axis=1).reshape(columns, nd, width)
    everyone = exchange(jnp.transpose(grads, (1, 0, 2)))
    adapter_grad = place(
        ids - owner_index * held, everyone.reshape(ids.shape[0], rank, width), held
    )
    frozen = dot(loss_sensitivity, weight, 1, 1).astype(jnp.bfloat16)
    frozen = lax.optimization_barrier(frozen).astype(jnp.float32)
    input_token_gradient = (frozen + adapter_scale * dot(low_out, down, 1, 0)).astype(jnp.bfloat16)
    return (input_token_gradient, adapter_grad)


def solution(mesh):
    return jax.shard_map(
        local,
        mesh=mesh,
        in_specs=(
            P(("group", "dp", "adapter"), None),
            P(("group", "dp", "adapter"), None),
            P("dp", None),
            P("adapter", None, "dp"),
            P(("group", "dp", "adapter")),
            P(("group", "dp", "adapter")),
        ),
        out_specs=(P(("group", "dp", "adapter"), None), P(("group", "adapter"), None, "dp")),
        check_vma=False,
    )
```

```python
import functools

import jax
import jax.numpy as jnp
from jax import lax
from jax.experimental import pallas as pl
from jax.experimental.pallas import tpu as pltpu
from jax.sharding import PartitionSpec as P

BLK = 128

adapter_scale = 2.0
MESH = pl.DeviceIdType.MESH
VMEM_LIMIT = 48 * 1024 * 1024


def remote(src, dst, send, recv, **where):
    return pltpu.make_async_remote_copy(
        src_ref=src, dst_ref=dst, send_sem=send, recv_sem=recv, device_id=where, device_id_type=MESH
    )


def greet(peers):
    barrier = pltpu.get_barrier_semaphore()
    nd = lax.axis_size("dp")
    me = lax.axis_index("dp")

    @pl.loop(1, nd)
    def _(o):
        pl.semaphore_signal(barrier, inc=1, device_id={"dp": lax.rem(me + o, nd)}, device_id_type=MESH)

    for peer in peers:
        pl.semaphore_signal(barrier, inc=1, device_id=peer, device_id_type=MESH)
    pl.semaphore_wait(barrier, nd - 1 + len(peers))


def fetch_kernel(
    nb, ids, cat, weight, fetched, gathered, pieces, from_core, from_x,
    s1, r1, s2, r2, s3, r3, sz, rz, sx, rx, sy, ry, sc, rc, local_sem,
):
    nd = lax.axis_size("dp")
    me = lax.axis_index("dp")
    g = lax.axis_index("group")
    a = lax.axis_index("adapter")
    x, c = a // 2, a % 2
    core = x * 2 + (1 - c)
    other = (1 - x) * 2 + c
    held, rank, _ = cat.shape
    greet([{"adapter": core}, {"adapter": other}, {"group": 1 - g}])

    def w_z(o):
        return remote(weight.at[c, g, x], gathered.at[me, c, g, x], sz.at[o], rz.at[o], dp=lax.rem(me + o, nd))

    def w_x(o):
        s = lax.rem(me + nd - o, nd)
        return remote(gathered.at[s, c, g, x], gathered.at[s, c, g, x], sx.at[o], rx.at[o], adapter=other)

    def w_y(o):
        s = lax.rem(me + nd - o, nd)
        return remote(gathered.at[s, c, g], gathered.at[s, c, g], sy.at[o], ry.at[o], group=1 - g)

    def w_c(o):
        s = lax.rem(me + nd - o, nd)
        return remote(gathered.at[s, c], gathered.at[s, c], sc.at[o], rc.at[o], adapter=core)

    def f_core(o):
        d = lax.rem(me + o, nd)
        return remote(pieces.at[d, 1 - c], from_core.at[d], s1.at[o], r1.at[o], adapter=core)

    def f_x(o):
        d = lax.rem(me + o, nd)
        return remote(pieces.at[d, c, 1 - x], from_x.at[d], s2.at[o], r2.at[o], adapter=other)

    def f_z(o):
        d = lax.rem(me + o, nd)
        return remote(pieces.at[d, c, x], fetched.at[me], s3.at[o], r3.at[o], dp=d)

    @pl.loop(1, nd)
    def _(o):
        w_z(o).start()

    own = pltpu.make_async_copy(weight, gathered.at[me], local_sem.at[0])
    own.start()

    @pl.loop(0, nd)
    def _(i):
        o = lax.rem(i + 1, nd)
        d = lax.rem(me + o, nd)

        @pl.loop(0, 4)
        def _(q):
            xx, cc = q // 2, q % 2
            for k in range(nb):
                local_id = ids[(d * 4 + q) * nb + k] - a * held
                valid = (local_id >= 0) & (local_id < held)
                row = cat[jnp.clip(local_id, 0, held - 1)]
                pieces[d, cc, xx, k * rank : (k + 1) * rank, :] = jnp.where(valid, row, jnp.zeros_like(row))

        f_core(o).start()

    @pl.loop(0, nd)
    def _(i):
        o = lax.rem(i + 1, nd)
        d = lax.rem(me + o, nd)
        f_core(o).wait_recv()
        pieces[d, c] += from_core[d]
        f_x(o).start()

    def x_done(o):
        d = lax.rem(me + o, nd)
        f_x(o).wait_recv()
        pieces[d, c, x] += from_x[d]

    @pl.loop(1, nd)
    def _(o):
        x_done(o)
        f_z(o).start()
        w_z(o).wait_recv()
        w_x(o).start()

    x_done(0)
    mine = pltpu.make_async_copy(pieces.at[me, c, x], fetched.at[me], local_sem.at[1])
    mine.start()

    @pl.loop(1, nd)
    def _(o):
        w_x(o).wait_recv()
        w_y(o).start()

    @pl.loop(1, nd)
    def _(o):
        w_y(o).wait_recv()
        w_c(o).start()

    @pl.loop(1, nd)
    def _(o):
        f_z(o).wait()
        w_z(o).wait_send()
        w_x(o).wait_send()
        w_y(o).wait_send()
        w_c(o).wait()

    @pl.loop(0, nd)
    def _(o):
        f_core(o).wait_send()
        f_x(o).wait_send()

    own.wait()
    mine.wait()


def fetch(ids, catalog, weight, nd, nb):
    held, rank, width = catalog.shape
    rows, kv = weight.shape
    weight = weight.reshape(2, 2, 2, rows // 8, kv)
    dma = pltpu.SemaphoreType.DMA((nd,))
    return pl.pallas_call(
        functools.partial(fetch_kernel, nb),
        out_shape=(
            jax.ShapeDtypeStruct((nd, nb * rank, width), jnp.bfloat16),
            jax.ShapeDtypeStruct((nd, 2, 2, 2, rows // 8, kv), jnp.bfloat16),
        ),
        in_specs=[
            pl.BlockSpec(memory_space=pltpu.SMEM),
            pl.BlockSpec(memory_space=pltpu.VMEM),
            pl.BlockSpec(memory_space=pl.ANY),
        ],
        out_specs=(pl.BlockSpec(memory_space=pl.ANY), pl.BlockSpec(memory_space=pl.ANY)),
        scratch_shapes=[
            pltpu.VMEM((nd, 2, 2, nb * rank, width), jnp.bfloat16),
            pltpu.VMEM((nd, 2, nb * rank, width), jnp.bfloat16),
            pltpu.VMEM((nd, nb * rank, width), jnp.bfloat16),
        ]
        + [dma] * 14
        + [pltpu.SemaphoreType.DMA((2,))],
        compiler_params=pltpu.CompilerParams(
            collective_id=0, has_side_effects=True, vmem_limit_bytes=VMEM_LIMIT
        ),
    )(ids, catalog, weight)


def exchange_kernel(grads, out, sz, rz, sx, rx, sc, rc, local_sem):
    nd = lax.axis_size("dp")
    me = lax.axis_index("dp")
    a = lax.axis_index("adapter")
    x, c = a // 2, a % 2
    core = x * 2 + (1 - c)
    other = (1 - x) * 2 + c
    greet([{"adapter": core}, {"adapter": other}])

    def g_z(o):
        d = lax.rem(me + o, nd)
        return remote(grads.at[d], out.at[me, x, c], sz.at[o], rz.at[o], dp=d)

    def g_x(o):
        s = lax.rem(me + nd - o, nd)
        return remote(out.at[s, x, c], out.at[s, x, c], sx.at[o], rx.at[o], adapter=other)

    def g_c(o):
        s = lax.rem(me + nd - o, nd)
        return remote(out.at[s, :, c], out.at[s, :, c], sc.at[o], rc.at[o], adapter=core)

    @pl.loop(1, nd)
    def _(o):
        g_z(o).start()

    own = pltpu.make_async_copy(grads.at[me], out.at[me, x, c], local_sem)
    own.start()
    own.wait()
    g_x(0).start()

    @pl.loop(1, nd)
    def _(o):
        g_z(o).wait_recv()
        g_x(o).start()

    @pl.loop(0, nd)
    def _(o):
        g_x(o).wait_recv()
        g_c(o).start()

    @pl.loop(1, nd)
    def _(o):
        g_z(o).wait_send()

    @pl.loop(0, nd)
    def _(o):
        g_x(o).wait_send()
        g_c(o).wait()


def exchange(grads):
    nd, rows, width = grads.shape
    dma = pltpu.SemaphoreType.DMA((nd,))
    return pl.pallas_call(
        exchange_kernel,
        out_shape=jax.ShapeDtypeStruct((nd, 2, 2, rows, width), jnp.bfloat16),
        in_specs=[pl.BlockSpec(memory_space=pl.ANY)],
        out_specs=pl.BlockSpec(memory_space=pl.ANY),
        scratch_shapes=[dma] * 6 + [pltpu.SemaphoreType.DMA],
        compiler_params=pltpu.CompilerParams(
            collective_id=1, has_side_effects=True, vmem_limit_bytes=VMEM_LIMIT
        ),
    )(grads)


def whole_kernel(
    nb, choice, cat_in, weight, tokens_in, cotangent, owned, gradient, out, spread,
    cat, tokens, ids, pieces, from_core, from_x, fetched, gathered, frozen, factors, grads,
    s1, r1, s2, r2, s3, r3, sz, rz, sx, rx, sy, ry, sc, rc, gsz, grz, gsx, grx, gsc, grc, ssa, rsa, ssb, rsb, local_sem,
):
    nd = lax.axis_size("dp")
    me = lax.axis_index("dp")
    g = lax.axis_index("group")
    a = lax.axis_index("adapter")
    x, c = a // 2, a % 2
    core = x * 2 + (1 - c)
    other = (1 - x) * 2 + c
    held, rank, width = cat.shape
    model_width = tokens.shape[1]
    shard = model_width // nd
    across = (1 - x) * 2 + (1 - c)
    greet([{"adapter": core}, {"adapter": other}, {"adapter": across}, {"group": 1 - g}])

    def after(o):
        return lax.rem(me + o, nd)

    def before(o):
        return lax.rem(me + nd - o, nd)

    def w_z(o):
        return remote(weight.at[c, g, x], gathered.at[me, c, g, x], sz.at[o], rz.at[o], dp=after(o))

    def w_x(o):
        block = gathered.at[before(o), c, g, x]
        return remote(block, block, sx.at[o], rx.at[o], adapter=other)

    def w_y(o):
        block = gathered.at[before(o), c, g]
        return remote(block, block, sy.at[o], ry.at[o], group=1 - g)

    def w_c(o):
        block = gathered.at[before(o), c]
        return remote(block, block, sc.at[o], rc.at[o], adapter=core)

    def f_core(o):
        d = after(o)
        return remote(pieces.at[d, 1 - c], from_core.at[d], s1.at[o], r1.at[o], adapter=core)

    def f_x(o):
        d = after(o)
        return remote(pieces.at[d, c, 1 - x], from_x.at[d], s2.at[o], r2.at[o], adapter=other)

    def f_z(o):
        d = after(o)
        return remote(pieces.at[d, c, x], fetched.at[me], s3.at[o], r3.at[o], dp=d)

    def g_z(o):
        d = after(o)
        return remote(grads.at[d], out.at[me, x, c], gsz.at[o], grz.at[o], dp=d)

    def g_x(o):
        block = out.at[before(o), x, c]
        return remote(block, block, gsx.at[o], grx.at[o], adapter=other)

    def g_c(o):
        block = out.at[before(o), :, c]
        return remote(block, block, gsc.at[o], grc.at[o], adapter=core)

    def i_z(o):
        return remote(choice, spread.at[me, a], ssa.at[o], rsa.at[o], dp=after(o))

    def i_a(k):
        block = spread.at[:, a]
        return remote(block, block, ssb.at[k], rsb.at[k], adapter=lax.rem(a + k, 4))

    def dot(lhs, rhs, left, right):
        return lax.dot_general(
            lhs, rhs, (((left,), (right,)), ((), ())), preferred_element_type=jnp.float32
        )

    def freeze(s):
        rows = gathered[s].reshape(shard, gathered.shape[-1])
        frozen[s] = dot(cotangent[...], rows, 1, 1).astype(jnp.bfloat16)

    @pl.loop(1, nd)
    def _(o):
        i_z(o).start()

    @pl.loop(1, nd)
    def _(o):
        w_z(o).start()

    load_cat = pltpu.make_async_copy(cat_in, cat, local_sem.at[2])
    load_cat.start()
    load_tokens = pltpu.make_async_copy(tokens_in, tokens, local_sem.at[3])
    load_tokens.start()
    spread[me, a] = choice[...]

    own = pltpu.make_async_copy(weight, gathered.at[me], local_sem.at[0])
    own.start()

    @pl.loop(1, nd)
    def _(o):
        i_z(o).wait_recv()

    @pl.loop(1, 4)
    def _(k):
        i_a(k).start()

    load_cat.wait()

    @pl.loop(1, 4)
    def _(k):
        i_a(k).wait_recv()

    to_scalar = pltpu.make_async_copy(spread, ids, local_sem.at[4])
    to_scalar.start()
    to_scalar.wait()

    @pl.loop(0, nd)
    def _(i):
        o = lax.rem(i + 1, nd)
        d = after(o)

        @pl.loop(0, 4)
        def _(q):
            xx, cc = q // 2, q % 2
            for k in range(nb):
                local_id = ids[d, q, 0, k] - a * held
                valid = (local_id >= 0) & (local_id < held)
                row = cat[jnp.clip(local_id, 0, held - 1)]
                pieces[d, cc, xx, k * rank : (k + 1) * rank, :] = jnp.where(valid, row, jnp.zeros_like(row))

        f_core(o).start()

    @pl.loop(0, nd)
    def _(i):
        o = lax.rem(i + 1, nd)
        d = after(o)
        f_core(o).wait_recv()
        pieces[d, c] += from_core[d]
        f_x(o).start()

    def x_done(o):
        d = after(o)
        f_x(o).wait_recv()
        pieces[d, c, x] += from_x[d]

    @pl.loop(1, nd)
    def _(o):
        x_done(o)
        f_z(o).start()
        w_z(o).wait_recv()
        w_x(o).start()

    x_done(0)
    fetched[me] = pieces[me, c, x]
    own.wait()
    freeze(me)
    w_x(1).wait_recv()
    w_y(1).start()

    @pl.loop(1, nd)
    def _(o):
        f_z(o).wait_recv()

    for j in range(nd):
        factors[:, j * width : (j + 1) * width] = fetched[j]
    load_tokens.wait()
    mask = owned[...] > 0
    low_out = dot(cotangent[...], factors[:, model_width:], 1, 1)
    low_out = jnp.where(mask, low_out, 0.0).astype(jnp.bfloat16)
    low_in = dot(tokens[...], factors[:, :model_width], 1, 1)
    low_in = jnp.where(mask, low_in, 0.0).astype(jnp.bfloat16)
    for j in range(nd):
        inner = min(max(model_width - j * width, 0), width)
        if inner:
            part = dot(low_out, tokens[:, j * width : j * width + inner], 0, 0)
            grads[j, :, :inner] = (adapter_scale * part).astype(jnp.bfloat16)
        if inner < width:
            start = j * width + inner - model_width
            part = dot(low_in, cotangent[:, start : start + width - inner], 0, 0)
            grads[j, :, inner:] = (adapter_scale * part).astype(jnp.bfloat16)

    @pl.loop(1, nd)
    def _(o):
        g_z(o).start()

    mine = pltpu.make_async_copy(grads.at[me], out.at[me, x, c], local_sem.at[1])
    mine.start()
    mine.wait()
    g_x(0).start()

    @pl.loop(2, nd)
    def _(o):
        w_x(o).wait_recv()
        w_y(o).start()

    @pl.loop(1, nd)
    def _(o):
        g_z(o).wait_recv()
        g_x(o).start()

    w_y(1).wait_recv()
    w_c(1).start()

    @pl.loop(0, nd)
    def _(o):
        g_x(o).wait_recv()
        g_c(o).start()

    @pl.loop(2, nd)
    def _(o):
        w_y(o).wait_recv()
        w_c(o).start()

    @pl.loop(1, nd)
    def _(o):
        w_c(o).wait_recv()
        freeze(before(o))

    for s in range(nd):
        columns = slice(s * shard, (s + 1) * shard)
        extra = dot(low_out, factors[:, columns], 1, 0)
        gradient[:, columns] = (frozen[s].astype(jnp.float32) + adapter_scale * extra).astype(jnp.bfloat16)

    @pl.loop(1, nd)
    def _(o):
        i_z(o).wait_send()
        f_z(o).wait_send()
        w_z(o).wait_send()
        w_x(o).wait_send()
        w_y(o).wait_send()
        w_c(o).wait_send()
        g_z(o).wait_send()

    @pl.loop(0, nd)
    def _(o):
        f_core(o).wait_send()
        f_x(o).wait_send()
        g_x(o).wait_send()
        g_c(o).wait()

    @pl.loop(1, 4)
    def _(k):
        i_a(k).wait_send()


def whole(choice, catalog, weight, tokens, cotangent, owned, nd, nb):
    held, rank, width = catalog.shape
    rows, kv = weight.shape
    columns = nb * rank
    weight = weight.reshape(2, 2, 2, rows // 8, kv)
    dma = pltpu.SemaphoreType.DMA((nd,))
    vmem = pl.BlockSpec(memory_space=pltpu.VMEM)
    anywhere = pl.BlockSpec(memory_space=pl.ANY)
    return pl.pallas_call(
        functools.partial(whole_kernel, nb),
        out_shape=(
            jax.ShapeDtypeStruct(tokens.shape, jnp.bfloat16),
            jax.ShapeDtypeStruct((nd, 2, 2, columns, width), jnp.bfloat16),
            jax.ShapeDtypeStruct((nd, 4) + choice.shape, jnp.int32),
        ),
        in_specs=[vmem, anywhere, anywhere, anywhere, vmem, vmem],
        out_specs=(vmem, anywhere, vmem),
        scratch_shapes=[
            pltpu.VMEM(catalog.shape, jnp.bfloat16),
            pltpu.VMEM(tokens.shape, jnp.bfloat16),
            pltpu.SMEM((nd, 4) + choice.shape, jnp.int32),
            pltpu.VMEM((nd, 2, 2, columns, width), jnp.bfloat16),
            pltpu.VMEM((nd, 2, columns, width), jnp.bfloat16),
            pltpu.VMEM((nd, columns, width), jnp.bfloat16),
            pltpu.VMEM((nd, columns, width), jnp.bfloat16),
            pltpu.VMEM((nd, 2, 2, 2, rows // 8, kv), jnp.bfloat16),
            pltpu.VMEM((nd, tokens.shape[0], rows), jnp.bfloat16),
            pltpu.VMEM((columns, nd * width), jnp.bfloat16),
            pltpu.VMEM((nd, columns, width), jnp.bfloat16),
        ]
        + [dma] * 22 + [pltpu.SemaphoreType.DMA((4,))] * 2
        + [pltpu.SemaphoreType.DMA((5,))],
        compiler_params=pltpu.CompilerParams(
            collective_id=2, has_side_effects=True, vmem_limit_bytes=VMEM_LIMIT
        ),
    )(choice, catalog, weight, tokens, cotangent, owned)


def place_kernel(nb, ids, rows, out, head, following):
    count, rank, width = out.shape
    step = pl.program_id(0)
    held = count * pl.num_programs(0)
    base = lax.axis_index("adapter") * held

    @pl.when(step == 0)
    def _():
        @pl.loop(0, held, unroll=8)
        def _(i):
            head[i] = -1

        @pl.loop(0, ids.shape[0])
        def _(device):
            for k in range(nb):
                target = ids[device, k] - base

                @pl.when((target >= 0) & (target < held))
                def _():
                    following[device * nb + k] = head[target]
                    head[target] = device * nb + k

    @pl.loop(0, count)
    def _(i):
        first = head[step * count + i]

        @pl.when(first < 0)
        def _():
            out[i] = jnp.zeros((rank, width), jnp.float32)

        @pl.when(first >= 0)
        def _():
            out[i] = rows[first].astype(jnp.float32)

            def add(s):
                out[i] += rows[s].astype(jnp.float32)
                return following[s]

            lax.while_loop(lambda s: s >= 0, add, following[first])


def place(ids, rows, held, nb):
    total, rank, width = rows.shape
    step = 16
    return pl.pallas_call(
        functools.partial(place_kernel, nb),
        out_shape=jax.ShapeDtypeStruct((held, rank, width), jnp.float32),
        grid_spec=pltpu.PrefetchScalarGridSpec(
            num_scalar_prefetch=1,
            grid=(held // step,),
            in_specs=[pl.BlockSpec((total, rank, width), lambda i, ids: (0, 0, 0))],
            out_specs=pl.BlockSpec((step, rank, width), lambda i, ids: (i, 0, 0)),
            scratch_shapes=[pltpu.SMEM((held,), jnp.int32), pltpu.SMEM((total,), jnp.int32)],
        ),
        compiler_params=pltpu.CompilerParams(vmem_limit_bytes=VMEM_LIMIT),
    )(ids, rows)


def local(
    layer_activation_matrix,
    loss_sensitivity,
    fixed_projection_matrix,
    plugin_factor_matrices,
    element_slot_position,
    segment_plugin_choice,
):
    token_count, model_width = layer_activation_matrix.shape
    block_count = segment_plugin_choice.shape[0]
    held, rank, width = plugin_factor_matrices.shape
    nd = lax.axis_size("dp")
    columns = block_count * rank
    owned = (element_slot_position // BLK)[:, None] == (jnp.arange(columns) // rank)[None, :]
    if width % 128 == 0 and model_width // nd % 128 == 0:
        choice = jnp.pad(segment_plugin_choice[None, :], ((0, 7), (0, 128 - block_count)))
        input_token_gradient, everyone, spread = whole(
            choice,
            plugin_factor_matrices,
            fixed_projection_matrix,
            layer_activation_matrix,
            loss_sensitivity,
            owned.astype(jnp.float32),
            nd,
            block_count,
        )
        ids = spread[:, :, 0, :].reshape(nd * 4, 128)
        everyone = everyone.reshape(nd * 4 * block_count, rank, width)
        return (input_token_gradient, place(ids, everyone, held, block_count))
    ids = lax.all_gather(segment_plugin_choice, ("dp", "adapter"), axis=0, tiled=True)
    fetched, weight = fetch(ids, plugin_factor_matrices, fixed_projection_matrix, nd, block_count)
    weight = weight.reshape(model_width, loss_sensitivity.shape[1])
    factors = jnp.transpose(fetched, (1, 0, 2)).reshape(columns, nd * width)
    down, up = factors[:, :model_width], factors[:, model_width:]

    def dot(lhs, rhs, left, right):
        return lax.dot_general(
            lhs, rhs, (((left,), (right,)), ((), ())), preferred_element_type=jnp.float32
        )

    low_in = jnp.where(owned, dot(layer_activation_matrix, down, 1, 1).astype(jnp.bfloat16), 0)
    low_out = jnp.where(owned, dot(loss_sensitivity, up, 1, 1).astype(jnp.bfloat16), 0)
    down_grad = (adapter_scale * dot(low_out, layer_activation_matrix, 0, 0)).astype(jnp.bfloat16)
    up_grad = (adapter_scale * dot(low_in, loss_sensitivity, 0, 0)).astype(jnp.bfloat16)
    grads = jnp.concatenate([down_grad, up_grad], axis=1).reshape(columns, nd, width)
    everyone = exchange(jnp.transpose(grads, (1, 0, 2)))
    adapter_grad = place(
        ids.reshape(nd * 4, block_count), everyone.reshape(ids.shape[0], rank, width), held, block_count
    )
    frozen = dot(loss_sensitivity, weight, 1, 1).astype(jnp.bfloat16)
    frozen = lax.optimization_barrier(frozen).astype(jnp.float32)
    input_token_gradient = (frozen + adapter_scale * dot(low_out, down, 1, 0)).astype(jnp.bfloat16)
    return (input_token_gradient, adapter_grad)


def solution(mesh):
    return jax.shard_map(
        local,
        mesh=mesh,
        in_specs=(
            P(("group", "dp", "adapter"), None),
            P(("group", "dp", "adapter"), None),
            P("dp", None),
            P("adapter", None, "dp"),
            P(("group", "dp", "adapter")),
            P(("group", "dp", "adapter")),
        ),
        out_specs=(P(("group", "dp", "adapter"), None), P(("group", "adapter"), None, "dp")),
        check_vma=False,
    )
```

```python
import functools

import jax
import jax.numpy as jnp
from jax import lax
from jax.experimental import pallas as pl
from jax.experimental.pallas import tpu as pltpu
from jax.sharding import PartitionSpec as P

BLK = 128

adapter_scale = 2.0
MESH = pl.DeviceIdType.MESH
VMEM_LIMIT = 48 * 1024 * 1024


def remote(src, dst, send, recv, **where):
    return pltpu.make_async_remote_copy(
        src_ref=src, dst_ref=dst, send_sem=send, recv_sem=recv, device_id=where, device_id_type=MESH
    )


def greet(peers):
    barrier = pltpu.get_barrier_semaphore()
    nd = lax.axis_size("dp")
    me = lax.axis_index("dp")

    @pl.loop(1, nd)
    def _(o):
        pl.semaphore_signal(barrier, inc=1, device_id={"dp": lax.rem(me + o, nd)}, device_id_type=MESH)

    for peer in peers:
        pl.semaphore_signal(barrier, inc=1, device_id=peer, device_id_type=MESH)
    pl.semaphore_wait(barrier, nd - 1 + len(peers))


def fetch_kernel(
    nb, ids, cat, weight, fetched, gathered, pieces, from_core, from_x,
    s1, r1, s2, r2, s3, r3, sz, rz, sx, rx, sy, ry, sc, rc, local_sem,
):
    nd = lax.axis_size("dp")
    me = lax.axis_index("dp")
    g = lax.axis_index("group")
    a = lax.axis_index("adapter")
    x, c = a // 2, a % 2
    core = x * 2 + (1 - c)
    other = (1 - x) * 2 + c
    held, rank, _ = cat.shape
    greet([{"adapter": core}, {"adapter": other}, {"group": 1 - g}])

    def w_z(o):
        return remote(weight.at[c, g, x], gathered.at[me, c, g, x], sz.at[o], rz.at[o], dp=lax.rem(me + o, nd))

    def w_x(o):
        s = lax.rem(me + nd - o, nd)
        return remote(gathered.at[s, c, g, x], gathered.at[s, c, g, x], sx.at[o], rx.at[o], adapter=other)

    def w_y(o):
        s = lax.rem(me + nd - o, nd)
        return remote(gathered.at[s, c, g], gathered.at[s, c, g], sy.at[o], ry.at[o], group=1 - g)

    def w_c(o):
        s = lax.rem(me + nd - o, nd)
        return remote(gathered.at[s, c], gathered.at[s, c], sc.at[o], rc.at[o], adapter=core)

    def f_core(o):
        d = lax.rem(me + o, nd)
        return remote(pieces.at[d, 1 - c], from_core.at[d], s1.at[o], r1.at[o], adapter=core)

    def f_x(o):
        d = lax.rem(me + o, nd)
        return remote(pieces.at[d, c, 1 - x], from_x.at[d], s2.at[o], r2.at[o], adapter=other)

    def f_z(o):
        d = lax.rem(me + o, nd)
        return remote(pieces.at[d, c, x], fetched.at[me], s3.at[o], r3.at[o], dp=d)

    @pl.loop(1, nd)
    def _(o):
        w_z(o).start()

    own = pltpu.make_async_copy(weight, gathered.at[me], local_sem.at[0])
    own.start()

    @pl.loop(0, nd)
    def _(i):
        o = lax.rem(i + 1, nd)
        d = lax.rem(me + o, nd)

        @pl.loop(0, 4)
        def _(q):
            xx, cc = q // 2, q % 2
            for k in range(nb):
                local_id = ids[(d * 4 + q) * nb + k] - a * held
                valid = (local_id >= 0) & (local_id < held)
                row = cat[jnp.clip(local_id, 0, held - 1)]
                pieces[d, cc, xx, k * rank : (k + 1) * rank, :] = jnp.where(valid, row, jnp.zeros_like(row))

        f_core(o).start()

    @pl.loop(0, nd)
    def _(i):
        o = lax.rem(i + 1, nd)
        d = lax.rem(me + o, nd)
        f_core(o).wait_recv()
        pieces[d, c] += from_core[d]
        f_x(o).start()

    def x_done(o):
        d = lax.rem(me + o, nd)
        f_x(o).wait_recv()
        pieces[d, c, x] += from_x[d]

    @pl.loop(1, nd)
    def _(o):
        x_done(o)
        f_z(o).start()
        w_z(o).wait_recv()
        w_x(o).start()

    x_done(0)
    mine = pltpu.make_async_copy(pieces.at[me, c, x], fetched.at[me], local_sem.at[1])
    mine.start()

    @pl.loop(1, nd)
    def _(o):
        w_x(o).wait_recv()
        w_y(o).start()

    @pl.loop(1, nd)
    def _(o):
        w_y(o).wait_recv()
        w_c(o).start()

    @pl.loop(1, nd)
    def _(o):
        f_z(o).wait()
        w_z(o).wait_send()
        w_x(o).wait_send()
        w_y(o).wait_send()
        w_c(o).wait()

    @pl.loop(0, nd)
    def _(o):
        f_core(o).wait_send()
        f_x(o).wait_send()

    own.wait()
    mine.wait()


def fetch(ids, catalog, weight, nd, nb):
    held, rank, width = catalog.shape
    rows, kv = weight.shape
    weight = weight.reshape(2, 2, 2, rows // 8, kv)
    dma = pltpu.SemaphoreType.DMA((nd,))
    return pl.pallas_call(
        functools.partial(fetch_kernel, nb),
        out_shape=(
            jax.ShapeDtypeStruct((nd, nb * rank, width), jnp.bfloat16),
            jax.ShapeDtypeStruct((nd, 2, 2, 2, rows // 8, kv), jnp.bfloat16),
        ),
        in_specs=[
            pl.BlockSpec(memory_space=pltpu.SMEM),
            pl.BlockSpec(memory_space=pltpu.VMEM),
            pl.BlockSpec(memory_space=pl.ANY),
        ],
        out_specs=(pl.BlockSpec(memory_space=pl.ANY), pl.BlockSpec(memory_space=pl.ANY)),
        scratch_shapes=[
            pltpu.VMEM((nd, 2, 2, nb * rank, width), jnp.bfloat16),
            pltpu.VMEM((nd, 2, nb * rank, width), jnp.bfloat16),
            pltpu.VMEM((nd, nb * rank, width), jnp.bfloat16),
        ]
        + [dma] * 14
        + [pltpu.SemaphoreType.DMA((2,))],
        compiler_params=pltpu.CompilerParams(
            collective_id=0, has_side_effects=True, vmem_limit_bytes=VMEM_LIMIT
        ),
    )(ids, catalog, weight)


def exchange_kernel(grads, out, sz, rz, sx, rx, sc, rc, local_sem):
    nd = lax.axis_size("dp")
    me = lax.axis_index("dp")
    a = lax.axis_index("adapter")
    x, c = a // 2, a % 2
    core = x * 2 + (1 - c)
    other = (1 - x) * 2 + c
    greet([{"adapter": core}, {"adapter": other}])

    def g_z(o):
        d = lax.rem(me + o, nd)
        return remote(grads.at[d], out.at[me, x, c], sz.at[o], rz.at[o], dp=d)

    def g_x(o):
        s = lax.rem(me + nd - o, nd)
        return remote(out.at[s, x, c], out.at[s, x, c], sx.at[o], rx.at[o], adapter=other)

    def g_c(o):
        s = lax.rem(me + nd - o, nd)
        return remote(out.at[s, :, c], out.at[s, :, c], sc.at[o], rc.at[o], adapter=core)

    @pl.loop(1, nd)
    def _(o):
        g_z(o).start()

    own = pltpu.make_async_copy(grads.at[me], out.at[me, x, c], local_sem)
    own.start()
    own.wait()
    g_x(0).start()

    @pl.loop(1, nd)
    def _(o):
        g_z(o).wait_recv()
        g_x(o).start()

    @pl.loop(0, nd)
    def _(o):
        g_x(o).wait_recv()
        g_c(o).start()

    @pl.loop(1, nd)
    def _(o):
        g_z(o).wait_send()

    @pl.loop(0, nd)
    def _(o):
        g_x(o).wait_send()
        g_c(o).wait()


def exchange(grads):
    nd, rows, width = grads.shape
    dma = pltpu.SemaphoreType.DMA((nd,))
    return pl.pallas_call(
        exchange_kernel,
        out_shape=jax.ShapeDtypeStruct((nd, 2, 2, rows, width), jnp.bfloat16),
        in_specs=[pl.BlockSpec(memory_space=pl.ANY)],
        out_specs=pl.BlockSpec(memory_space=pl.ANY),
        scratch_shapes=[dma] * 6 + [pltpu.SemaphoreType.DMA],
        compiler_params=pltpu.CompilerParams(
            collective_id=1, has_side_effects=True, vmem_limit_bytes=VMEM_LIMIT
        ),
    )(grads)


def whole_kernel(
    nb, choice, cat_in, weight, tokens_in, cotangent, owned, gradient, out, spread,
    cat, tokens, ids, pieces, from_core, from_x, fetched, gathered, frozen, factors, grads,
    s1, r1, s2, r2, s3, r3, sz, rz, sx, rx, sy, ry, sc, rc, gsz, grz, gsx, grx, gsc, grc, ssa, rsa, ssb, rsb, local_sem,
):
    nd = lax.axis_size("dp")
    me = lax.axis_index("dp")
    g = lax.axis_index("group")
    a = lax.axis_index("adapter")
    x, c = a // 2, a % 2
    core = x * 2 + (1 - c)
    other = (1 - x) * 2 + c
    held, rank, width = cat.shape
    model_width = tokens.shape[1]
    shard = model_width // nd
    across = (1 - x) * 2 + (1 - c)
    greet([{"adapter": core}, {"adapter": other}, {"adapter": across}, {"group": 1 - g}])

    def after(o):
        return lax.rem(me + o, nd)

    def before(o):
        return lax.rem(me + nd - o, nd)

    def w_z(o):
        return remote(weight.at[c, g, x], gathered.at[me, c, g, x], sz.at[o], rz.at[o], dp=after(o))

    def w_x(o):
        block = gathered.at[before(o), c, g, x]
        return remote(block, block, sx.at[o], rx.at[o], adapter=other)

    def w_y(o):
        block = gathered.at[before(o), c, g]
        return remote(block, block, sy.at[o], ry.at[o], group=1 - g)

    def w_c(o):
        block = gathered.at[before(o), c]
        return remote(block, block, sc.at[o], rc.at[o], adapter=core)

    def f_core(o):
        d = after(o)
        return remote(pieces.at[d, 1 - c], from_core.at[d], s1.at[o], r1.at[o], adapter=core)

    def f_x(o):
        d = after(o)
        return remote(pieces.at[d, c, 1 - x], from_x.at[d], s2.at[o], r2.at[o], adapter=other)

    def f_z(o):
        d = after(o)
        return remote(pieces.at[d, c, x], fetched.at[me], s3.at[o], r3.at[o], dp=d)

    def g_z(o):
        d = after(o)
        return remote(grads.at[d], out.at[me, x, c], gsz.at[o], grz.at[o], dp=d)

    def g_x(o):
        block = out.at[before(o), x, c]
        return remote(block, block, gsx.at[o], grx.at[o], adapter=other)

    def g_c(o):
        block = out.at[before(o), :, c]
        return remote(block, block, gsc.at[o], grc.at[o], adapter=core)

    def i_z(o):
        return remote(choice, spread.at[me, a], ssa.at[o], rsa.at[o], dp=after(o))

    def i_a(k):
        block = spread.at[:, a]
        return remote(block, block, ssb.at[k], rsb.at[k], adapter=lax.rem(a + k, 4))

    def dot(lhs, rhs, left, right):
        return lax.dot_general(
            lhs, rhs, (((left,), (right,)), ((), ())), preferred_element_type=jnp.float32
        )

    def freeze(s):
        rows = gathered[s].reshape(shard, gathered.shape[-1])
        frozen[s] = dot(cotangent[...], rows, 1, 1).astype(jnp.bfloat16)

    @pl.loop(1, nd)
    def _(o):
        i_z(o).start()

    @pl.loop(1, nd)
    def _(o):
        w_z(o).start()

    load_cat = pltpu.make_async_copy(cat_in, cat, local_sem.at[2])
    load_cat.start()
    load_tokens = pltpu.make_async_copy(tokens_in, tokens, local_sem.at[3])
    load_tokens.start()
    spread[me, a] = choice[...]

    own = pltpu.make_async_copy(weight, gathered.at[me], local_sem.at[0])
    own.start()

    @pl.loop(1, nd)
    def _(o):
        i_z(o).wait_recv()

    @pl.loop(1, 4)
    def _(k):
        i_a(k).start()

    load_cat.wait()

    @pl.loop(1, 4)
    def _(k):
        i_a(k).wait_recv()

    to_scalar = pltpu.make_async_copy(spread, ids, local_sem.at[4])
    to_scalar.start()
    to_scalar.wait()

    @pl.loop(0, nd)
    def _(i):
        o = lax.rem(i + 1, nd)
        d = after(o)

        @pl.loop(0, 4)
        def _(q):
            xx, cc = q // 2, q % 2
            for k in range(nb):
                local_id = ids[d, q, 0, k] - a * held
                valid = (local_id >= 0) & (local_id < held)
                row = cat[jnp.clip(local_id, 0, held - 1)]
                pieces[d, cc, xx, k * rank : (k + 1) * rank, :] = jnp.where(valid, row, jnp.zeros_like(row))

        f_core(o).start()

    @pl.loop(0, nd)
    def _(i):
        o = lax.rem(i + 1, nd)
        d = after(o)
        f_core(o).wait_recv()
        pieces[d, c] += from_core[d]
        f_x(o).start()

    def x_done(o):
        d = after(o)
        f_x(o).wait_recv()
        pieces[d, c, x] += from_x[d]

    @pl.loop(1, nd)
    def _(o):
        x_done(o)
        f_z(o).start()
        w_z(o).wait_recv()
        w_x(o).start()

    x_done(0)
    fetched[me] = pieces[me, c, x]
    own.wait()
    freeze(me)

    @pl.loop(1, nd)
    def _(o):
        w_x(o).wait_recv()
        w_y(o).start()

    @pl.loop(1, nd)
    def _(o):
        f_z(o).wait_recv()

    for j in range(nd):
        factors[:, j * width : (j + 1) * width] = fetched[j]
    load_tokens.wait()
    mask = owned[...] > 0
    low_out = dot(cotangent[...], factors[:, model_width:], 1, 1)
    low_out = jnp.where(mask, low_out, 0.0).astype(jnp.bfloat16)
    low_in = dot(tokens[...], factors[:, :model_width], 1, 1)
    low_in = jnp.where(mask, low_in, 0.0).astype(jnp.bfloat16)
    for j in range(nd):
        inner = min(max(model_width - j * width, 0), width)
        if inner:
            part = dot(low_out, tokens[:, j * width : j * width + inner], 0, 0)
            grads[j, :, :inner] = (adapter_scale * part).astype(jnp.bfloat16)
        if inner < width:
            start = j * width + inner - model_width
            part = dot(low_in, cotangent[:, start : start + width - inner], 0, 0)
            grads[j, :, inner:] = (adapter_scale * part).astype(jnp.bfloat16)

    @pl.loop(1, nd)
    def _(o):
        g_z(o).start()

    mine = pltpu.make_async_copy(grads.at[me], out.at[me, x, c], local_sem.at[1])
    mine.start()
    mine.wait()
    g_x(0).start()

    @pl.loop(1, nd)
    def _(o):
        g_z(o).wait_recv()
        g_x(o).start()

    w_y(1).wait_recv()
    w_c(1).start()

    @pl.loop(0, nd)
    def _(o):
        g_x(o).wait_recv()
        g_c(o).start()

    @pl.loop(2, nd)
    def _(o):
        w_y(o).wait_recv()
        w_c(o).start()

    @pl.loop(1, nd)
    def _(o):
        w_c(o).wait_recv()
        freeze(before(o))

    for s in range(nd):
        columns = slice(s * shard, (s + 1) * shard)
        extra = dot(low_out, factors[:, columns], 1, 0)
        gradient[:, columns] = (frozen[s].astype(jnp.float32) + adapter_scale * extra).astype(jnp.bfloat16)

    @pl.loop(1, nd)
    def _(o):
        i_z(o).wait_send()
        f_z(o).wait_send()
        w_z(o).wait_send()
        w_x(o).wait_send()
        w_y(o).wait_send()
        w_c(o).wait_send()
        g_z(o).wait_send()

    @pl.loop(0, nd)
    def _(o):
        f_core(o).wait_send()
        f_x(o).wait_send()
        g_x(o).wait_send()
        g_c(o).wait()

    @pl.loop(1, 4)
    def _(k):
        i_a(k).wait_send()


def whole(choice, catalog, weight, tokens, cotangent, owned, nd, nb):
    held, rank, width = catalog.shape
    rows, kv = weight.shape
    columns = nb * rank
    weight = weight.reshape(2, 2, 2, rows // 8, kv)
    dma = pltpu.SemaphoreType.DMA((nd,))
    vmem = pl.BlockSpec(memory_space=pltpu.VMEM)
    anywhere = pl.BlockSpec(memory_space=pl.ANY)
    return pl.pallas_call(
        functools.partial(whole_kernel, nb),
        out_shape=(
            jax.ShapeDtypeStruct(tokens.shape, jnp.bfloat16),
            jax.ShapeDtypeStruct((nd, 2, 2, columns, width), jnp.bfloat16),
            jax.ShapeDtypeStruct((nd, 4) + choice.shape, jnp.int32),
        ),
        in_specs=[vmem, anywhere, anywhere, anywhere, vmem, vmem],
        out_specs=(vmem, anywhere, vmem),
        scratch_shapes=[
            pltpu.VMEM(catalog.shape, jnp.bfloat16),
            pltpu.VMEM(tokens.shape, jnp.bfloat16),
            pltpu.SMEM((nd, 4) + choice.shape, jnp.int32),
            pltpu.VMEM((nd, 2, 2, columns, width), jnp.bfloat16),
            pltpu.VMEM((nd, 2, columns, width), jnp.bfloat16),
            pltpu.VMEM((nd, columns, width), jnp.bfloat16),
            pltpu.VMEM((nd, columns, width), jnp.bfloat16),
            pltpu.VMEM((nd, 2, 2, 2, rows // 8, kv), jnp.bfloat16),
            pltpu.VMEM((nd, tokens.shape[0], rows), jnp.bfloat16),
            pltpu.VMEM((columns, nd * width), jnp.bfloat16),
            pltpu.VMEM((nd, columns, width), jnp.bfloat16),
        ]
        + [dma] * 22 + [pltpu.SemaphoreType.DMA((4,))] * 2
        + [pltpu.SemaphoreType.DMA((5,))],
        compiler_params=pltpu.CompilerParams(
            collective_id=2, has_side_effects=True, vmem_limit_bytes=VMEM_LIMIT
        ),
    )(choice, catalog, weight, tokens, cotangent, owned)


def place_kernel(nb, ids, rows, out, head, following):
    count, rank, width = out.shape
    step = pl.program_id(0)
    held = count * pl.num_programs(0)
    base = lax.axis_index("adapter") * held

    @pl.when(step == 0)
    def _():
        @pl.loop(0, held, unroll=8)
        def _(i):
            head[i] = -1

        @pl.loop(0, ids.shape[0])
        def _(device):
            for k in range(nb):
                target = ids[device, k] - base

                @pl.when((target >= 0) & (target < held))
                def _():
                    following[device * nb + k] = head[target]
                    head[target] = device * nb + k

    @pl.loop(0, count)
    def _(i):
        first = head[step * count + i]

        @pl.when(first < 0)
        def _():
            out[i] = jnp.zeros((rank, width), jnp.float32)

        @pl.when(first >= 0)
        def _():
            out[i] = rows[first].astype(jnp.float32)

            def add(s):
                out[i] += rows[s].astype(jnp.float32)
                return following[s]

            lax.while_loop(lambda s: s >= 0, add, following[first])


def place(ids, rows, held, nb):
    total, rank, width = rows.shape
    step = 16
    return pl.pallas_call(
        functools.partial(place_kernel, nb),
        out_shape=jax.ShapeDtypeStruct((held, rank, width), jnp.float32),
        grid_spec=pltpu.PrefetchScalarGridSpec(
            num_scalar_prefetch=1,
            grid=(held // step,),
            in_specs=[pl.BlockSpec((total, rank, width), lambda i, ids: (0, 0, 0))],
            out_specs=pl.BlockSpec((step, rank, width), lambda i, ids: (i, 0, 0)),
            scratch_shapes=[pltpu.SMEM((held,), jnp.int32), pltpu.SMEM((total,), jnp.int32)],
        ),
        compiler_params=pltpu.CompilerParams(vmem_limit_bytes=VMEM_LIMIT),
    )(ids, rows)


def local(
    layer_activation_matrix,
    loss_sensitivity,
    fixed_projection_matrix,
    plugin_factor_matrices,
    element_slot_position,
    segment_plugin_choice,
):
    token_count, model_width = layer_activation_matrix.shape
    block_count = segment_plugin_choice.shape[0]
    held, rank, width = plugin_factor_matrices.shape
    nd = lax.axis_size("dp")
    columns = block_count * rank
    owned = (element_slot_position // BLK)[:, None] == (jnp.arange(columns) // rank)[None, :]
    if width % 128 == 0 and model_width // nd % 128 == 0:
        choice = jnp.pad(segment_plugin_choice[None, :], ((0, 7), (0, 128 - block_count)))
        input_token_gradient, everyone, spread = whole(
            choice,
            plugin_factor_matrices,
            fixed_projection_matrix,
            layer_activation_matrix,
            loss_sensitivity,
            owned.astype(jnp.float32),
            nd,
            block_count,
        )
        ids = spread[:, :, 0, :].reshape(nd * 4, 128)
        everyone = everyone.reshape(nd * 4 * block_count, rank, width)
        return (input_token_gradient, place(ids, everyone, held, block_count))
    ids = lax.all_gather(segment_plugin_choice, ("dp", "adapter"), axis=0, tiled=True)
    fetched, weight = fetch(ids, plugin_factor_matrices, fixed_projection_matrix, nd, block_count)
    weight = weight.reshape(model_width, loss_sensitivity.shape[1])
    factors = jnp.transpose(fetched, (1, 0, 2)).reshape(columns, nd * width)
    down, up = factors[:, :model_width], factors[:, model_width:]

    def dot(lhs, rhs, left, right):
        return lax.dot_general(
            lhs, rhs, (((left,), (right,)), ((), ())), preferred_element_type=jnp.float32
        )

    low_in = jnp.where(owned, dot(layer_activation_matrix, down, 1, 1).astype(jnp.bfloat16), 0)
    low_out = jnp.where(owned, dot(loss_sensitivity, up, 1, 1).astype(jnp.bfloat16), 0)
    down_grad = (adapter_scale * dot(low_out, layer_activation_matrix, 0, 0)).astype(jnp.bfloat16)
    up_grad = (adapter_scale * dot(low_in, loss_sensitivity, 0, 0)).astype(jnp.bfloat16)
    grads = jnp.concatenate([down_grad, up_grad], axis=1).reshape(columns, nd, width)
    everyone = exchange(jnp.transpose(grads, (1, 0, 2)))
    adapter_grad = place(
        ids.reshape(nd * 4, block_count), everyone.reshape(ids.shape[0], rank, width), held, block_count
    )
    frozen = dot(loss_sensitivity, weight, 1, 1).astype(jnp.bfloat16)
    frozen = lax.optimization_barrier(frozen).astype(jnp.float32)
    input_token_gradient = (frozen + adapter_scale * dot(low_out, down, 1, 0)).astype(jnp.bfloat16)
    return (input_token_gradient, adapter_grad)


def solution(mesh):
    return jax.shard_map(
        local,
        mesh=mesh,
        in_specs=(
            P(("group", "dp", "adapter"), None),
            P(("group", "dp", "adapter"), None),
            P("dp", None),
            P("adapter", None, "dp"),
            P(("group", "dp", "adapter")),
            P(("group", "dp", "adapter")),
        ),
        out_specs=(P(("group", "dp", "adapter"), None), P(("group", "adapter"), None, "dp")),
        check_vma=False,
    )
```

```python
import functools

import jax
import jax.numpy as jnp
from jax import lax
from jax.experimental import pallas as pl
from jax.experimental.pallas import tpu as pltpu
from jax.sharding import PartitionSpec as P

BLK = 128

adapter_scale = 2.0
MESH = pl.DeviceIdType.MESH
VMEM_LIMIT = 48 * 1024 * 1024


def remote(src, dst, send, recv, **where):
    return pltpu.make_async_remote_copy(
        src_ref=src, dst_ref=dst, send_sem=send, recv_sem=recv, device_id=where, device_id_type=MESH
    )


def greet(peers):
    barrier = pltpu.get_barrier_semaphore()
    nd = lax.axis_size("dp")
    me = lax.axis_index("dp")

    @pl.loop(1, nd)
    def _(o):
        pl.semaphore_signal(barrier, inc=1, device_id={"dp": lax.rem(me + o, nd)}, device_id_type=MESH)

    for peer in peers:
        pl.semaphore_signal(barrier, inc=1, device_id=peer, device_id_type=MESH)
    pl.semaphore_wait(barrier, nd - 1 + len(peers))


def fetch_kernel(
    nb, ids, cat, weight, fetched, gathered, pieces, from_core, from_x,
    s1, r1, s2, r2, s3, r3, sz, rz, sx, rx, sy, ry, sc, rc, local_sem,
):
    nd = lax.axis_size("dp")
    me = lax.axis_index("dp")
    g = lax.axis_index("group")
    a = lax.axis_index("adapter")
    x, c = a // 2, a % 2
    core = x * 2 + (1 - c)
    other = (1 - x) * 2 + c
    held, rank, _ = cat.shape
    greet([{"adapter": core}, {"adapter": other}, {"group": 1 - g}])

    def w_z(o):
        return remote(weight.at[c, g, x], gathered.at[me, c, g, x], sz.at[o], rz.at[o], dp=lax.rem(me + o, nd))

    def w_x(o):
        s = lax.rem(me + nd - o, nd)
        return remote(gathered.at[s, c, g, x], gathered.at[s, c, g, x], sx.at[o], rx.at[o], adapter=other)

    def w_y(o):
        s = lax.rem(me + nd - o, nd)
        return remote(gathered.at[s, c, g], gathered.at[s, c, g], sy.at[o], ry.at[o], group=1 - g)

    def w_c(o):
        s = lax.rem(me + nd - o, nd)
        return remote(gathered.at[s, c], gathered.at[s, c], sc.at[o], rc.at[o], adapter=core)

    def f_core(o):
        d = lax.rem(me + o, nd)
        return remote(pieces.at[d, 1 - c], from_core.at[d], s1.at[o], r1.at[o], adapter=core)

    def f_x(o):
        d = lax.rem(me + o, nd)
        return remote(pieces.at[d, c, 1 - x], from_x.at[d], s2.at[o], r2.at[o], adapter=other)

    def f_z(o):
        d = lax.rem(me + o, nd)
        return remote(pieces.at[d, c, x], fetched.at[me], s3.at[o], r3.at[o], dp=d)

    @pl.loop(1, nd)
    def _(o):
        w_z(o).start()

    own = pltpu.make_async_copy(weight, gathered.at[me], local_sem.at[0])
    own.start()

    @pl.loop(0, nd)
    def _(i):
        o = lax.rem(i + 1, nd)
        d = lax.rem(me + o, nd)

        @pl.loop(0, 4)
        def _(q):
            xx, cc = q // 2, q % 2
            for k in range(nb):
                local_id = ids[(d * 4 + q) * nb + k] - a * held
                valid = (local_id >= 0) & (local_id < held)
                row = cat[jnp.clip(local_id, 0, held - 1)]
                pieces[d, cc, xx, k * rank : (k + 1) * rank, :] = jnp.where(valid, row, jnp.zeros_like(row))

        f_core(o).start()

    @pl.loop(0, nd)
    def _(i):
        o = lax.rem(i + 1, nd)
        d = lax.rem(me + o, nd)
        f_core(o).wait_recv()
        pieces[d, c] += from_core[d]
        f_x(o).start()

    def x_done(o):
        d = lax.rem(me + o, nd)
        f_x(o).wait_recv()
        pieces[d, c, x] += from_x[d]

    @pl.loop(1, nd)
    def _(o):
        x_done(o)
        f_z(o).start()
        w_z(o).wait_recv()
        w_x(o).start()

    x_done(0)
    mine = pltpu.make_async_copy(pieces.at[me, c, x], fetched.at[me], local_sem.at[1])
    mine.start()

    @pl.loop(1, nd)
    def _(o):
        w_x(o).wait_recv()
        w_y(o).start()

    @pl.loop(1, nd)
    def _(o):
        w_y(o).wait_recv()
        w_c(o).start()

    @pl.loop(1, nd)
    def _(o):
        f_z(o).wait()
        w_z(o).wait_send()
        w_x(o).wait_send()
        w_y(o).wait_send()
        w_c(o).wait()

    @pl.loop(0, nd)
    def _(o):
        f_core(o).wait_send()
        f_x(o).wait_send()

    own.wait()
    mine.wait()


def fetch(ids, catalog, weight, nd, nb):
    held, rank, width = catalog.shape
    rows, kv = weight.shape
    weight = weight.reshape(2, 2, 2, rows // 8, kv)
    dma = pltpu.SemaphoreType.DMA((nd,))
    return pl.pallas_call(
        functools.partial(fetch_kernel, nb),
        out_shape=(
            jax.ShapeDtypeStruct((nd, nb * rank, width), jnp.bfloat16),
            jax.ShapeDtypeStruct((nd, 2, 2, 2, rows // 8, kv), jnp.bfloat16),
        ),
        in_specs=[
            pl.BlockSpec(memory_space=pltpu.SMEM),
            pl.BlockSpec(memory_space=pltpu.VMEM),
            pl.BlockSpec(memory_space=pl.ANY),
        ],
        out_specs=(pl.BlockSpec(memory_space=pl.ANY), pl.BlockSpec(memory_space=pl.ANY)),
        scratch_shapes=[
            pltpu.VMEM((nd, 2, 2, nb * rank, width), jnp.bfloat16),
            pltpu.VMEM((nd, 2, nb * rank, width), jnp.bfloat16),
            pltpu.VMEM((nd, nb * rank, width), jnp.bfloat16),
        ]
        + [dma] * 14
        + [pltpu.SemaphoreType.DMA((2,))],
        compiler_params=pltpu.CompilerParams(
            collective_id=0, has_side_effects=True, vmem_limit_bytes=VMEM_LIMIT
        ),
    )(ids, catalog, weight)


def exchange_kernel(grads, out, sz, rz, sx, rx, sc, rc, local_sem):
    nd = lax.axis_size("dp")
    me = lax.axis_index("dp")
    a = lax.axis_index("adapter")
    x, c = a // 2, a % 2
    core = x * 2 + (1 - c)
    other = (1 - x) * 2 + c
    greet([{"adapter": core}, {"adapter": other}])

    def g_z(o):
        d = lax.rem(me + o, nd)
        return remote(grads.at[d], out.at[me, x, c], sz.at[o], rz.at[o], dp=d)

    def g_x(o):
        s = lax.rem(me + nd - o, nd)
        return remote(out.at[s, x, c], out.at[s, x, c], sx.at[o], rx.at[o], adapter=other)

    def g_c(o):
        s = lax.rem(me + nd - o, nd)
        return remote(out.at[s, :, c], out.at[s, :, c], sc.at[o], rc.at[o], adapter=core)

    @pl.loop(1, nd)
    def _(o):
        g_z(o).start()

    own = pltpu.make_async_copy(grads.at[me], out.at[me, x, c], local_sem)
    own.start()
    own.wait()
    g_x(0).start()

    @pl.loop(1, nd)
    def _(o):
        g_z(o).wait_recv()
        g_x(o).start()

    @pl.loop(0, nd)
    def _(o):
        g_x(o).wait_recv()
        g_c(o).start()

    @pl.loop(1, nd)
    def _(o):
        g_z(o).wait_send()

    @pl.loop(0, nd)
    def _(o):
        g_x(o).wait_send()
        g_c(o).wait()


def exchange(grads):
    nd, rows, width = grads.shape
    dma = pltpu.SemaphoreType.DMA((nd,))
    return pl.pallas_call(
        exchange_kernel,
        out_shape=jax.ShapeDtypeStruct((nd, 2, 2, rows, width), jnp.bfloat16),
        in_specs=[pl.BlockSpec(memory_space=pl.ANY)],
        out_specs=pl.BlockSpec(memory_space=pl.ANY),
        scratch_shapes=[dma] * 6 + [pltpu.SemaphoreType.DMA],
        compiler_params=pltpu.CompilerParams(
            collective_id=1, has_side_effects=True, vmem_limit_bytes=VMEM_LIMIT
        ),
    )(grads)


def whole_kernel(
    nb, choice, cat_in, weight, tokens_in, cotangent, owned, gradient, out, spread,
    cat, tokens, ids, pieces, from_core, from_x, fetched, gathered, frozen, factors, grads,
    s1, r1, s2, r2, s3, r3, sz, rz, sx, rx, sy, ry, sc, rc, gsz, grz, gsx, grx, gsc, grc, ssa, rsa, ssb, rsb, local_sem,
):
    nd = lax.axis_size("dp")
    me = lax.axis_index("dp")
    g = lax.axis_index("group")
    a = lax.axis_index("adapter")
    x, c = a // 2, a % 2
    core = x * 2 + (1 - c)
    other = (1 - x) * 2 + c
    held, rank, width = cat.shape
    model_width = tokens.shape[1]
    shard = model_width // nd
    across = (1 - x) * 2 + (1 - c)
    greet([{"adapter": core}, {"adapter": other}, {"adapter": across}, {"group": 1 - g}])

    def after(o):
        return lax.rem(me + o, nd)

    def before(o):
        return lax.rem(me + nd - o, nd)

    def w_z(o):
        return remote(weight.at[c, g, x], gathered.at[me, c, g, x], sz.at[o], rz.at[o], dp=after(o))

    def w_x(o):
        block = gathered.at[before(o), c, g, x]
        return remote(block, block, sx.at[o], rx.at[o], adapter=other)

    def w_y(o):
        block = gathered.at[before(o), c, g]
        return remote(block, block, sy.at[o], ry.at[o], group=1 - g)

    def w_c(o):
        block = gathered.at[before(o), c]
        return remote(block, block, sc.at[o], rc.at[o], adapter=core)

    def f_core(o):
        d = after(o)
        return remote(pieces.at[d, 1 - c], from_core.at[d], s1.at[o], r1.at[o], adapter=core)

    def f_x(o):
        d = after(o)
        return remote(pieces.at[d, c, 1 - x], from_x.at[d], s2.at[o], r2.at[o], adapter=other)

    def f_z(o):
        d = after(o)
        return remote(pieces.at[d, c, x], fetched.at[me], s3.at[o], r3.at[o], dp=d)

    def g_z(o):
        d = after(o)
        return remote(grads.at[d], out.at[me, x, c], gsz.at[o], grz.at[o], dp=d)

    def g_x(o):
        block = out.at[before(o), x, c]
        return remote(block, block, gsx.at[o], grx.at[o], adapter=other)

    def g_c(o):
        block = out.at[before(o), :, c]
        return remote(block, block, gsc.at[o], grc.at[o], adapter=core)

    def i_z(o):
        return remote(choice, spread.at[me, a], ssa.at[o], rsa.at[o], dp=after(o))

    def i_a(k):
        block = spread.at[:, a]
        return remote(block, block, ssb.at[k], rsb.at[k], adapter=lax.rem(a + k, 4))

    def dot(lhs, rhs, left, right):
        return lax.dot_general(
            lhs, rhs, (((left,), (right,)), ((), ())), preferred_element_type=jnp.float32
        )

    def freeze(s):
        rows = gathered[s].reshape(shard, gathered.shape[-1])
        frozen[s] = dot(cotangent[...], rows, 1, 1).astype(jnp.bfloat16)

    @pl.loop(1, nd)
    def _(o):
        i_z(o).start()

    w_z(1).start()
    w_z(nd - 1).start()

    load_cat = pltpu.make_async_copy(cat_in, cat, local_sem.at[2])
    load_cat.start()
    load_tokens = pltpu.make_async_copy(tokens_in, tokens, local_sem.at[3])
    load_tokens.start()
    spread[me, a] = choice[...]

    own = pltpu.make_async_copy(weight, gathered.at[me], local_sem.at[0])
    own.start()

    @pl.loop(1, nd)
    def _(o):
        i_z(o).wait_recv()

    @pl.loop(1, 4)
    def _(k):
        i_a(k).start()

    load_cat.wait()

    @pl.loop(1, 4)
    def _(k):
        i_a(k).wait_recv()

    to_scalar = pltpu.make_async_copy(spread, ids, local_sem.at[4])
    to_scalar.start()
    to_scalar.wait()

    @pl.loop(0, nd)
    def _(i):
        o = lax.rem(i + 1, nd)
        d = after(o)

        @pl.loop(0, 4)
        def _(q):
            xx, cc = q // 2, q % 2
            for k in range(nb):
                local_id = ids[d, q, 0, k] - a * held
                valid = (local_id >= 0) & (local_id < held)
                row = cat[jnp.clip(local_id, 0, held - 1)]
                pieces[d, cc, xx, k * rank : (k + 1) * rank, :] = jnp.where(valid, row, jnp.zeros_like(row))

        f_core(o).start()

    @pl.loop(0, nd)
    def _(i):
        o = lax.rem(i + 1, nd)
        d = after(o)
        f_core(o).wait_recv()
        pieces[d, c] += from_core[d]
        f_x(o).start()

    def x_done(o):
        d = after(o)
        f_x(o).wait_recv()
        pieces[d, c, x] += from_x[d]

    @pl.loop(1, nd)
    def _(o):
        x_done(o)
        f_z(o).start()

    @pl.loop(2, nd - 1)
    def _(o):
        w_z(o).start()

    w_z(1).wait_recv()
    w_x(1).start()
    w_z(nd - 1).wait_recv()
    w_x(nd - 1).start()
    x_done(0)
    fetched[me] = pieces[me, c, x]
    own.wait()
    freeze(me)
    w_x(1).wait_recv()
    w_y(1).start()

    @pl.loop(1, nd)
    def _(o):
        f_z(o).wait_recv()

    for j in range(nd):
        factors[:, j * width : (j + 1) * width] = fetched[j]
    load_tokens.wait()
    mask = owned[...] > 0
    low_out = dot(cotangent[...], factors[:, model_width:], 1, 1)
    low_out = jnp.where(mask, low_out, 0.0).astype(jnp.bfloat16)
    low_in = dot(tokens[...], factors[:, :model_width], 1, 1)
    low_in = jnp.where(mask, low_in, 0.0).astype(jnp.bfloat16)
    for j in range(nd):
        inner = min(max(model_width - j * width, 0), width)
        if inner:
            part = dot(low_out, tokens[:, j * width : j * width + inner], 0, 0)
            grads[j, :, :inner] = (adapter_scale * part).astype(jnp.bfloat16)
        if inner < width:
            start = j * width + inner - model_width
            part = dot(low_in, cotangent[:, start : start + width - inner], 0, 0)
            grads[j, :, inner:] = (adapter_scale * part).astype(jnp.bfloat16)

    @pl.loop(1, nd)
    def _(o):
        g_z(o).start()

    mine = pltpu.make_async_copy(grads.at[me], out.at[me, x, c], local_sem.at[1])
    mine.start()
    mine.wait()
    g_x(0).start()

    w_x(nd - 1).wait_recv()
    w_y(nd - 1).start()

    @pl.loop(2, nd - 1)
    def _(o):
        w_z(o).wait_recv()
        w_x(o).start()

    @pl.loop(2, nd - 1)
    def _(o):
        w_x(o).wait_recv()
        w_y(o).start()

    @pl.loop(1, nd)
    def _(o):
        g_z(o).wait_recv()
        g_x(o).start()

    w_y(1).wait_recv()
    w_c(1).start()

    @pl.loop(0, nd)
    def _(o):
        g_x(o).wait_recv()
        g_c(o).start()

    w_y(nd - 1).wait_recv()
    w_c(nd - 1).start()
    w_c(1).wait_recv()
    freeze(before(1))

    @pl.loop(2, nd - 1)
    def _(o):
        w_y(o).wait_recv()
        w_c(o).start()

    @pl.loop(2, nd)
    def _(o):
        w_c(o).wait_recv()
        freeze(before(o))

    for s in range(nd):
        columns = slice(s * shard, (s + 1) * shard)
        extra = dot(low_out, factors[:, columns], 1, 0)
        gradient[:, columns] = (frozen[s].astype(jnp.float32) + adapter_scale * extra).astype(jnp.bfloat16)

    @pl.loop(1, nd)
    def _(o):
        i_z(o).wait_send()
        f_z(o).wait_send()
        w_z(o).wait_send()
        w_x(o).wait_send()
        w_y(o).wait_send()
        w_c(o).wait_send()
        g_z(o).wait_send()

    @pl.loop(0, nd)
    def _(o):
        f_core(o).wait_send()
        f_x(o).wait_send()
        g_x(o).wait_send()
        g_c(o).wait()

    @pl.loop(1, 4)
    def _(k):
        i_a(k).wait_send()


def whole(choice, catalog, weight, tokens, cotangent, owned, nd, nb):
    held, rank, width = catalog.shape
    rows, kv = weight.shape
    columns = nb * rank
    weight = weight.reshape(2, 2, 2, rows // 8, kv)
    dma = pltpu.SemaphoreType.DMA((nd,))
    vmem = pl.BlockSpec(memory_space=pltpu.VMEM)
    anywhere = pl.BlockSpec(memory_space=pl.ANY)
    return pl.pallas_call(
        functools.partial(whole_kernel, nb),
        out_shape=(
            jax.ShapeDtypeStruct(tokens.shape, jnp.bfloat16),
            jax.ShapeDtypeStruct((nd, 2, 2, columns, width), jnp.bfloat16),
            jax.ShapeDtypeStruct((nd, 4) + choice.shape, jnp.int32),
        ),
        in_specs=[vmem, anywhere, anywhere, anywhere, vmem, vmem],
        out_specs=(vmem, anywhere, vmem),
        scratch_shapes=[
            pltpu.VMEM(catalog.shape, jnp.bfloat16),
            pltpu.VMEM(tokens.shape, jnp.bfloat16),
            pltpu.SMEM((nd, 4) + choice.shape, jnp.int32),
            pltpu.VMEM((nd, 2, 2, columns, width), jnp.bfloat16),
            pltpu.VMEM((nd, 2, columns, width), jnp.bfloat16),
            pltpu.VMEM((nd, columns, width), jnp.bfloat16),
            pltpu.VMEM((nd, columns, width), jnp.bfloat16),
            pltpu.VMEM((nd, 2, 2, 2, rows // 8, kv), jnp.bfloat16),
            pltpu.VMEM((nd, tokens.shape[0], rows), jnp.bfloat16),
            pltpu.VMEM((columns, nd * width), jnp.bfloat16),
            pltpu.VMEM((nd, columns, width), jnp.bfloat16),
        ]
        + [dma] * 22 + [pltpu.SemaphoreType.DMA((4,))] * 2
        + [pltpu.SemaphoreType.DMA((5,))],
        compiler_params=pltpu.CompilerParams(
            collective_id=2, has_side_effects=True, vmem_limit_bytes=VMEM_LIMIT
        ),
    )(choice, catalog, weight, tokens, cotangent, owned)


def place_kernel(nb, ids, rows, out, head, following):
    count, rank, width = out.shape
    step = pl.program_id(0)
    held = count * pl.num_programs(0)
    base = lax.axis_index("adapter") * held

    @pl.when(step == 0)
    def _():
        @pl.loop(0, held, unroll=8)
        def _(i):
            head[i] = -1

        @pl.loop(0, ids.shape[0])
        def _(device):
            for k in range(nb):
                target = ids[device, k] - base

                @pl.when((target >= 0) & (target < held))
                def _():
                    following[device * nb + k] = head[target]
                    head[target] = device * nb + k

    @pl.loop(0, count)
    def _(i):
        first = head[step * count + i]

        @pl.when(first < 0)
        def _():
            out[i] = jnp.zeros((rank, width), jnp.float32)

        @pl.when(first >= 0)
        def _():
            out[i] = rows[first].astype(jnp.float32)

            def add(s):
                out[i] += rows[s].astype(jnp.float32)
                return following[s]

            lax.while_loop(lambda s: s >= 0, add, following[first])


def place(ids, rows, held, nb):
    total, rank, width = rows.shape
    step = 16
    return pl.pallas_call(
        functools.partial(place_kernel, nb),
        out_shape=jax.ShapeDtypeStruct((held, rank, width), jnp.float32),
        grid_spec=pltpu.PrefetchScalarGridSpec(
            num_scalar_prefetch=1,
            grid=(held // step,),
            in_specs=[pl.BlockSpec((total, rank, width), lambda i, ids: (0, 0, 0))],
            out_specs=pl.BlockSpec((step, rank, width), lambda i, ids: (i, 0, 0)),
            scratch_shapes=[pltpu.SMEM((held,), jnp.int32), pltpu.SMEM((total,), jnp.int32)],
        ),
        compiler_params=pltpu.CompilerParams(vmem_limit_bytes=VMEM_LIMIT),
    )(ids, rows)


def local(
    layer_activation_matrix,
    loss_sensitivity,
    fixed_projection_matrix,
    plugin_factor_matrices,
    element_slot_position,
    segment_plugin_choice,
):
    token_count, model_width = layer_activation_matrix.shape
    block_count = segment_plugin_choice.shape[0]
    held, rank, width = plugin_factor_matrices.shape
    nd = lax.axis_size("dp")
    columns = block_count * rank
    owned = (element_slot_position // BLK)[:, None] == (jnp.arange(columns) // rank)[None, :]
    if nd > 2 and width % 128 == 0 and model_width // nd % 128 == 0:
        choice = jnp.pad(segment_plugin_choice[None, :], ((0, 7), (0, 128 - block_count)))
        input_token_gradient, everyone, spread = whole(
            choice,
            plugin_factor_matrices,
            fixed_projection_matrix,
            layer_activation_matrix,
            loss_sensitivity,
            owned.astype(jnp.float32),
            nd,
            block_count,
        )
        ids = spread[:, :, 0, :].reshape(nd * 4, 128)
        everyone = everyone.reshape(nd * 4 * block_count, rank, width)
        return (input_token_gradient, place(ids, everyone, held, block_count))
    ids = lax.all_gather(segment_plugin_choice, ("dp", "adapter"), axis=0, tiled=True)
    fetched, weight = fetch(ids, plugin_factor_matrices, fixed_projection_matrix, nd, block_count)
    weight = weight.reshape(model_width, loss_sensitivity.shape[1])
    factors = jnp.transpose(fetched, (1, 0, 2)).reshape(columns, nd * width)
    down, up = factors[:, :model_width], factors[:, model_width:]

    def dot(lhs, rhs, left, right):
        return lax.dot_general(
            lhs, rhs, (((left,), (right,)), ((), ())), preferred_element_type=jnp.float32
        )

    low_in = jnp.where(owned, dot(layer_activation_matrix, down, 1, 1).astype(jnp.bfloat16), 0)
    low_out = jnp.where(owned, dot(loss_sensitivity, up, 1, 1).astype(jnp.bfloat16), 0)
    down_grad = (adapter_scale * dot(low_out, layer_activation_matrix, 0, 0)).astype(jnp.bfloat16)
    up_grad = (adapter_scale * dot(low_in, loss_sensitivity, 0, 0)).astype(jnp.bfloat16)
    grads = jnp.concatenate([down_grad, up_grad], axis=1).reshape(columns, nd, width)
    everyone = exchange(jnp.transpose(grads, (1, 0, 2)))
    adapter_grad = place(
        ids.reshape(nd * 4, block_count), everyone.reshape(ids.shape[0], rank, width), held, block_count
    )
    frozen = dot(loss_sensitivity, weight, 1, 1).astype(jnp.bfloat16)
    frozen = lax.optimization_barrier(frozen).astype(jnp.float32)
    input_token_gradient = (frozen + adapter_scale * dot(low_out, down, 1, 0)).astype(jnp.bfloat16)
    return (input_token_gradient, adapter_grad)


def solution(mesh):
    return jax.shard_map(
        local,
        mesh=mesh,
        in_specs=(
            P(("group", "dp", "adapter"), None),
            P(("group", "dp", "adapter"), None),
            P("dp", None),
            P("adapter", None, "dp"),
            P(("group", "dp", "adapter")),
            P(("group", "dp", "adapter")),
        ),
        out_specs=(P(("group", "dp", "adapter"), None), P(("group", "adapter"), None, "dp")),
        check_vma=False,
    )
```
